128 devices in a mesh: dp: 16 (over x_hi, y, core), ctx: 8 (over x_lo, z).
Axes of the slice: x: 4 (x_hi: 2, x_lo: 2; x = x_hi * 2 + x_lo), y: 4, z: 4, core: 2. Of those that a mesh axis runs over, the one named last changes fastest.
Arguments:
- qkv: bfloat16 [16384, 3, 4096], P(('dp', 'ctx')), may hold values from -6 to 6
- short_filter: float32 [3, 3, 4096], P(None, None, 'ctx'), may hold values from -3 to 3
- inner_filter: float32 [7, 256], P(None, 'ctx'), may hold values from -2 to 2
- out_weight: bfloat16 [4096, 4096], P('dp', 'ctx'), may hold values from -0.09375 to 0.09375
- cotangent: bfloat16 [16384, 4096], P(('dp', 'ctx')), may hold values from -6 to 6
- order: int32 [16, 1024], P('dp'), may hold values from 0 to 1023, each once within a row
- lengths: int32 [16, 8], P('dp'), may hold values from 1 to 512, 1024 in all within a row
Outputs:
- mixed: bfloat16 [16384, 4096], P(('dp', 'ctx'))
- grad_qkv: bfloat16 [16384, 3, 4096], P(('dp', 'ctx'))
- grad_weight: float32 [4096, 4096], P('dp', 'ctx')
- grad_short: float32 [3, 3, 4096], P(None, None, 'ctx')
- grad_inner: float32 [7, 256], P(None, 'ctx')
The draws below stay inside these ranges and needn't reach their ends.
Inputs may be any that keep to these rules, and one draw needn't show every extreme that they name: `order`: each row is a permutation of the positions of one context. `lengths`: each row sums to 1024; its longest record is exactly 512.
All inputs are finite; a program needn't handle non-finite values.
Results may differ from the reference program's by a relative error of at most 0.017.
Values may be sent and summed in bfloat16 or wider, within the bound.
A program may use at most 128 MiB of HBM per device.

```python
import math
import jax
import jax.numpy as jnp
import numpy as np
from jax import lax

D = 4096
C = 4096
GROUP = 16
TAPS = 7
SHORT = 3
RECS = 8
G = 256
CTXLEN = 1024
MOSTLEN = 512
TOKENS = 16384
N_DP = 16
N_CTX = 8


def shard_levels(own_key, shape, pieces, low, largest):
    level, own = 1.0, jax.random.fold_in(own_key, 6)
    for position, parts in pieces:
        heights = jnp.exp(jax.random.uniform(jax.random.fold_in(own, position), (parts,), jnp.float32, low / len(pieces), largest / len(pieces)))
        level = level * jnp.repeat(heights, shape[position] // parts).reshape([-1 if axis == position else 1 for axis in range(len(shape))])
    return level


def split_up(count, total, bound, lean):
    loads = [(1 << 20) // math.isqrt(grade ** lean) + 1 for grade in range(2, count + 1)]
    spare, counts = total - bound - (count - 1), [1] * (count - 1)
    while spare > 0:
        movable = [i for i in range(count - 1) if counts[i] < bound]
        mass, left = sum([loads[i] for i in movable]), spare
        for i in movable:
            addition = min(bound - counts[i], max(1, left * loads[i] // mass), spare)
            counts[i] = counts[i] + addition
            spare = spare - addition
    return np.array([bound] + counts)


def uneven_parts(key, number_of, total, bound, slope):
    if number_of == 2:
        one = jax.random.randint(key, (), max(1, total - bound), min(bound, total - 1) + 1)
        return jnp.stack([one, total - one])
    sizes = jnp.asarray(split_up(number_of, total, bound, slope), jnp.int32)
    couples = (number_of - 1) // 2
    donor, sink = sizes[1:1 + 2 * couples:2], sizes[2:2 + 2 * couples:2]
    slack = jnp.minimum(donor - 1, bound - sink)
    shifted = jax.random.randint(jax.random.fold_in(key, 1), (couples,), 0, 1 << 20) % (slack + 1)
    sizes = sizes.at[1:1 + 2 * couples:2].set(donor - shifted).at[2:2 + 2 * couples:2].set(sink + shifted)
    return sizes[jax.random.permutation(jax.random.fold_in(key, 2), number_of)]


def scatter_about(rng, dims, scale, reach, shards=(), kind=jnp.bfloat16):
    values = jax.random.normal(rng, dims, jnp.float32) * scale
    if len(shards) > 0:
        values = shard_levels(rng, dims, shards, -0.22, 0.18) * values
    return jnp.clip(values, min=-reach, max=reach).astype(kind)


def setup_inputs(seed: int = 0) -> dict:
    key_of = jax.random.split(jax.random.key(seed), 8)
    return {
        "qkv": scatter_about(key_of[0], (TOKENS, 3, C), 1.0, 6.0, ((0, 128),)),
        "short_filter": scatter_about(key_of[1], (SHORT, 3, C), 0.6, 3.0, ((2, 8),), jnp.float32),
        "inner_filter": scatter_about(key_of[2], (TAPS, G), 0.4, 2.0, ((1, 8),), jnp.float32),
        "out_weight": scatter_about(key_of[3], (D, C), C ** -0.5, 0.09375, ((0, 16), (1, 8))),
        "cotangent": scatter_about(key_of[4], (TOKENS, D), 1.0, 6.0, ((0, 128),)),
        "order": jax.vmap(lambda own: jax.random.permutation(own, CTXLEN))(jax.random.split(key_of[5], N_DP)).reshape((N_DP, CTXLEN)).astype(jnp.int32),
        "lengths": jax.vmap(lambda own: uneven_parts(own, RECS, CTXLEN, MOSTLEN, 2))(jax.random.split(key_of[6], N_DP)).reshape((N_DP, RECS)).astype(jnp.int32),
    }


def record_start(lens, length):
    ends = jnp.cumsum(lens).astype(jnp.int32)
    places = jnp.arange(length, dtype=jnp.int32)
    chosen = jnp.where(ends[None, :] <= places[:, None], ends[None, :], jnp.int32(0))
    return jnp.max(chosen, axis=1)


def shift_down(x, t):
    if t == 0:
        return x
    return jnp.concatenate([jnp.zeros((t,) + x.shape[1:], x.dtype), x[:-t]], 0)


def shift_up(x, t):
    if t == 0:
        return x
    return jnp.concatenate([x[t:], jnp.zeros((t,) + x.shape[1:], x.dtype)], 0)


def masks_for(start, taps, extra):
    places = jnp.arange(start.shape[0], dtype=jnp.int32)
    result = []
    for t in range(taps):
        valid = jnp.where(places - t >= start, 1.0, 0.0).astype(jnp.float32)
        result.append(valid.reshape((-1,) + (1,) * extra))
    return result


def causal(x, taps, masks):
    total = jnp.zeros(x.shape, jnp.float32)
    for t in range(taps.shape[0]):
        total = total + taps[t] * masks[t] * shift_down(x, t)
    return total


def causal_back(d, taps, masks):
    total = jnp.zeros(d.shape, jnp.float32)
    for t in range(taps.shape[0]):
        total = total + taps[t] * shift_up(d * masks[t], t)
    return total


def tap_grads(d, x, masks, taps):
    rows = []
    for t in range(taps):
        rows.append(jnp.sum(d * masks[t] * shift_down(x, t), axis=0))
    return jnp.stack(rows, 0)


def reference(qkv, short_filter, inner_filter, out_weight, cotangent, order, lengths):
    streams = qkv.reshape(N_DP, CTXLEN, 3, C)
    grads_in = cotangent.reshape(N_DP, CTXLEN, D)
    inner_full = jnp.repeat(inner_filter, GROUP, axis=1)
    block = C // N_CTX

    def one(carry, item):
        acc_weight, acc_short, acc_inner = carry
        stored, grad_rows, perm, lens = item
        inverse = jnp.zeros((CTXLEN,), jnp.int32).at[perm].set(jnp.arange(CTXLEN, dtype=jnp.int32))
        start = record_start(lens, CTXLEN)
        masks3 = masks_for(start, SHORT, 2)
        masks7 = masks_for(start, TAPS, 1)
        upos = stored[inverse].astype(jnp.float32)
        feats = causal(upos, short_filter, masks3)
        query, keyed, value = feats[:, 0], feats[:, 1], feats[:, 2]
        inner_in = keyed * value
        mixed_w = causal(inner_in, inner_full, masks7)
        ypos = (query * mixed_w).astype(jnp.bfloat16)
        ystored = ypos[perm]
        total = jnp.zeros((CTXLEN, D), jnp.float32)
        for b in range(N_CTX):
            part = jnp.dot(ystored[:, b * block:(b + 1) * block], out_weight[:, b * block:(b + 1) * block].T, preferred_element_type=jnp.float32)
            part = lax.optimization_barrier(part.astype(jnp.bfloat16)).astype(jnp.float32)
            total = total + part
        out_rows = total.astype(jnp.bfloat16)
        dystored = jnp.dot(grad_rows, out_weight, preferred_element_type=jnp.float32)
        dypos = dystored[inverse]
        grad_w = jnp.dot(grad_rows.T, ystored, preferred_element_type=jnp.float32)
        d_w = dypos * query
        d_q = dypos * mixed_w
        d_z = causal_back(d_w, inner_full, masks7)
        d_inner = tap_grads(d_w, inner_in, masks7, TAPS).reshape(TAPS, G, GROUP).sum(-1)
        d_f = jnp.stack([d_q, d_z * value, d_z * keyed], 1)
        d_short = tap_grads(d_f, upos, masks3, SHORT)
        d_u = causal_back(d_f, short_filter, masks3)
        du_rows = d_u[perm].astype(jnp.bfloat16)
        return (acc_weight + grad_w, acc_short + d_short, acc_inner + d_inner), (out_rows, du_rows)

    init = (jnp.zeros((D, C), jnp.float32), jnp.zeros((SHORT, 3, C), jnp.float32), jnp.zeros((TAPS, G), jnp.float32))
    sums, outs = lax.scan(one, init, (streams, grads_in, order, lengths))
    mixed = outs[0].reshape(TOKENS, D)
    grad_qkv = outs[1].reshape(TOKENS, 3, C)
    return (mixed, grad_qkv, sums[0], sums[1], sums[2])
```

```python
import jax
import jax.numpy as jnp
from jax import lax
from jax.sharding import PartitionSpec as P
from jax.experimental import pallas as pl
from jax.experimental.pallas import tpu as pltpu

MESH = pl.DeviceIdType.MESH
F32 = jnp.float32
BF16 = jnp.bfloat16
GROUP = 16
L = 1024
CB = 512
HF = 2048
ROWS = 128
PAD = 16
STRIP = 64
A2A = ((0, 2), (1, 2), (1, 1), (1, 3), (0, 1), (0, 3), (1, 0))


def where_am_i():
    j = lax.axis_index("ctx")
    return j, j // 4, lax.rem(j, 4)


def peer(x, z, dx, dz):
    return lax.rem(x + dx, 2) * 4 + lax.rem(z + dz, 4)


def barrier(ids):
    sem = pltpu.get_barrier_semaphore()
    for d in ids:
        pl.semaphore_signal(sem, inc=1, device_id=d, device_id_type=MESH)
    pl.semaphore_wait(sem, len(ids))


def fill_masks(lens_ref, m_ref):
    p = lax.broadcasted_iota(jnp.int32, m_ref.shape, 0) - PAD
    good = (p > 0) & (p < L)
    end = jnp.int32(0)
    for k in range(lens_ref.shape[1]):
        end = end + lens_ref[0, k]
        good = good & (p != end)
    m_ref[...] = jnp.where(good, 1.0, 0.0).astype(F32)


def fill_gather(order_row_ref, out_ref):
    def step(i, c):
        r0 = pl.multiple_of(i * 128, 128)
        p = lax.broadcasted_iota(jnp.int32, (128, L), 0) + r0
        out_ref[pl.ds(r0, 128), :] = jnp.where(p == order_row_ref[...], 1.0, 0.0).astype(BF16)
        return c

    lax.fori_loop(0, L // 128, step, 0)


def fill_scatter(order_col_ref, out_ref):
    def step(i, c):
        r0 = pl.multiple_of(i * 128, 128)
        p = lax.broadcasted_iota(jnp.int32, (128, L), 1)
        out_ref[pl.ds(r0, 128), :] = jnp.where(p == order_col_ref[pl.ds(r0, 128), :], 1.0, 0.0).astype(BF16)
        return c

    lax.fori_loop(0, L // 128, step, 0)


def down(x, m):
    return pltpu.roll(x, 1, 0) * m


def up(x, m):
    return pltpu.roll(x * m, x.shape[0] - 1, 0)


def taps3(u, m, filt):
    u1 = down(u, m)
    u2 = down(u1, m)
    return filt[0] * u + filt[1] * u1 + filt[2] * u2, u1, u2


def front_kernel(
    qs, cot, order_row, order_col, lens, short, inner,
    upos, cotz, yout,
    arrived, perm, mask, ypos, ystored,
    a_s, a_r, c_s, c_r, l_s,
):
    j, x, z = where_am_i()
    xb = peer(x, z, 1, 0)
    zu, zd = peer(x, z, 0, 1), peer(x, z, 0, 3)
    barrier([{"ctx": peer(x, z, dx, dz)} for dx, dz in A2A])

    sends = []
    for n, (dx, dz) in enumerate(A2A):
        p = peer(x, z, dx, dz)
        c = pltpu.make_async_remote_copy(
            qs.at[p], arrived.at[pl.ds(j * ROWS, ROWS)], a_s.at[n], a_r.at[n], device_id={"ctx": p}, device_id_type=MESH
        )
        c.start()
        sends.append(c)
    own_q = pltpu.make_async_copy(qs.at[j], arrived.at[pl.ds(j * ROWS, ROWS)], l_s.at[0])
    own_q.start()
    mine = cot.at[:, pl.ds(x * HF, HF)]
    own_c = pltpu.make_async_copy(mine, cotz.at[x, z], l_s.at[1])
    own_c.start()

    fill_masks(lens, mask)
    fill_gather(order_row, perm)
    upos[pl.ds(0, PAD), :] = jnp.zeros((PAD, 3 * CB), BF16)
    upos[pl.ds(PAD + L, PAD), :] = jnp.zeros((PAD, 3 * CB), BF16)
    own_q.wait()
    for c in sends:
        c.wait_recv()

    def copy(src, dst, n, to):
        c = pltpu.make_async_remote_copy(src, dst, c_s.at[n], c_r.at[n], device_id={"ctx": to}, device_id_type=MESH)
        c.start()
        return c

    over = copy(cot.at[:, pl.ds((1 - x) * HF, HF)], cotz.at[x, z], 0, xb)
    u_own = copy(mine, cotz.at[x, z], 1, zu)
    d_own = copy(mine, cotz.at[x, z], 2, zd)

    def place(i, c):
        c0 = pl.multiple_of(i * 256, 256)
        upos[pl.ds(PAD, L), pl.ds(c0, 256)] = jnp.dot(
            perm[...], arrived[:, pl.ds(c0, 256)], preferred_element_type=F32
        ).astype(BF16)
        return c

    lax.fori_loop(0, 3 * CB // 256, place, 0)

    over.wait_recv()
    u_oth = copy(cotz.at[1 - x, z], cotz.at[1 - x, z], 3, zu)
    d_oth = copy(cotz.at[1 - x, z], cotz.at[1 - x, z], 4, zd)

    def forward(n, carry):
        c0 = pl.multiple_of(lax.rem(n, CB // 128) * 128, 128)
        r0 = pl.multiple_of((n // (CB // 128)) * STRIP, STRIP)
        m = mask[pl.ds(r0 + 8, STRIP + 8), :]
        feats = []
        for a in range(3):
            u = upos[pl.ds(r0, STRIP + PAD), pl.ds(a * CB + c0, 128)].astype(F32)[8:]
            filt = [short[pl.ds(t * 3 + a, 1), pl.ds(c0, 128)] for t in range(3)]
            feats.append(taps3(u, m, filt)[0])
        q, k, v = feats
        zt = k * v
        w = inner[pl.ds(0, 1), pl.ds(c0, 128)] * zt
        for t in range(1, 7):
            zt = down(zt, m)
            w = w + inner[pl.ds(t, 1), pl.ds(c0, 128)] * zt
        ypos[pl.ds(r0, STRIP), pl.ds(c0, 128)] = (q * w)[8:].astype(BF16)
        return carry

    lax.fori_loop(0, (CB // 128) * (L // STRIP), forward, 0)
    fill_scatter(order_col, perm)
    for h in range(2):
        cols = pl.ds(h * 256, 256)
        ystored[:, cols] = jnp.dot(perm[...], ypos[:, cols], preferred_element_type=F32).astype(BF16)
    y_x = copy(ystored, yout.at[:, pl.ds(x * CB, CB)], 7, xb)
    own_y = pltpu.make_async_copy(ystored, yout.at[:, pl.ds(x * CB, CB)], l_s.at[2])
    own_y.start()

    zul, zdl = lax.rem(z + 1, 4), lax.rem(z + 3, 4)
    u_own.wait_recv()
    d_own.wait_recv()
    u_oth.wait_recv()
    d_oth.wait_recv()
    on_u = copy(cotz.at[0, zdl], cotz.at[0, zdl], 5, zu)
    on_d = copy(cotz.at[1, zul], cotz.at[1, zul], 6, zd)
    for c in (on_u, on_d, y_x):
        c.wait()
    for c in (over, u_own, d_own, u_oth, d_oth):
        c.wait_send()
    for c in sends:
        c.wait_send()
    own_c.wait()
    own_y.wait()


def back_kernel(
    cotz, y, w2, upos, order_row, order_col, lens, short, inner,
    mixed, dugot, grads,
    perm, permt, mask, dysend, dyrecv, dystored, dypos, dupos, dusend,
    lhs, hold, own, first, direct, fwd, got1, got2, final, gacc, gall,
    d_s, d_r, r_s, r_r, q_s, q_r, g_s, g_r, l_s,
):
    j, x, z = where_am_i()
    i = lax.axis_index("dp")
    xb = peer(x, z, 1, 0)
    zu, zd = peer(x, z, 0, 1), peer(x, z, 0, 3)
    dps = [lax.rem(i + n, 16) for n in range(1, 16)]
    barrier([{"ctx": peer(x, z, dx, dz)} for dx, dz in A2A] + [{"dp": p} for p in dps])

    d_x = []
    for c in range(2):
        cols = pl.ds(c * 256, 256)

        def other(n, carry):
            r0 = pl.multiple_of(n * 256, 256)
            dysend[c, pl.ds(r0, 256), :] = jnp.dot(
                cotz[pl.ds(r0, 256), :], w2[1 - x, :, cols], preferred_element_type=F32
            ).astype(BF16)
            return carry

        lax.fori_loop(0, L // 256, other, 0)
        cp = pltpu.make_async_remote_copy(
            dysend.at[c], dyrecv.at[c], d_s.at[c], d_r.at[c], device_id={"ctx": xb}, device_id_type=MESH
        )
        cp.start()
        d_x.append(cp)

    def product(dz, put):
        zz = lax.rem(z + dz, 4)
        for a in range(2):
            lhs[pl.ds(a * ROWS, ROWS), :] = y[pl.ds(pl.multiple_of(a * 512 + zz * ROWS, ROWS), ROWS), :]

        def part(n, carry):
            f0 = pl.multiple_of(n * 256, 256)
            dims = (((1,), (1,)), ((), ()))
            val = lax.dot_general(
                lhs[:, pl.ds(0, CB)], w2[0, pl.ds(f0, 256), :], dims, preferred_element_type=F32
            ) + lax.dot_general(lhs[:, pl.ds(CB, CB)], w2[1, pl.ds(f0, 256), :], dims, preferred_element_type=F32)
            put(f0, val)
            return carry

        lax.fori_loop(0, HF // 256, part, 0)

    def copy(src, dst, n, to):
        c = pltpu.make_async_remote_copy(src, dst, r_s.at[n], r_r.at[n], device_id={"ctx": to}, device_id_type=MESH)
        c.start()
        return c

    def put_first(f0, val):
        first[0, :, pl.ds(f0, 256)] = val[:ROWS].astype(BF16)
        first[1, :, pl.ds(f0, 256)] = val[ROWS:].astype(BF16)

    product(2, put_first)
    s_u = copy(first.at[0], got1.at[0], 0, zu)
    s_d = copy(first.at[1], got1.at[1], 1, zd)

    def put_up(f0, val):
        hold[0, :, pl.ds(f0, 256)] = val[:ROWS]
        direct[0, :, pl.ds(f0, 256)] = val[ROWS:].astype(BF16)

    product(1, put_up)
    t_u = copy(direct.at[0], got2.at[0, 1], 2, zu)

    def put_down(f0, val):
        direct[1, :, pl.ds(f0, 256)] = val[:ROWS].astype(BF16)
        hold[1, :, pl.ds(f0, 256)] = val[ROWS:]

    product(3, put_down)
    t_d = copy(direct.at[1], got2.at[1, 0], 3, zd)

    fill_masks(lens, mask)
    fill_gather(order_row, perm)
    fill_scatter(order_col, permt)
    gacc[...] = jnp.zeros_like(gacc)

    def combine(a):
        def step(n, carry):
            r0 = pl.multiple_of(n * 16, 16)
            fwd[a, pl.ds(r0, 16), :] = (hold[a, pl.ds(r0, 16), :] + got1[a, pl.ds(r0, 16), :].astype(F32)).astype(BF16)
            return carry

        lax.fori_loop(0, ROWS // 16, step, 0)

    s_u.wait_recv()
    combine(0)
    f_u = copy(fwd.at[0], got2.at[0, 0], 4, zu)
    s_d.wait_recv()
    combine(1)
    f_d = copy(fwd.at[1], got2.at[1, 1], 5, zd)

    def put_own(f0, val):
        own[0, :, pl.ds(f0, 256)] = val[:ROWS]
        own[1, :, pl.ds(f0, 256)] = val[ROWS:]

    dypos[pl.ds(L, 8), :] = jnp.zeros((8, 256), F32)
    d_a = []
    for c in range(2):
        cols = pl.ds(c * 256, 256)
        d_x[c].wait_recv()

        def mine(n, carry):
            r0 = pl.multiple_of(n * 256, 256)
            val = jnp.dot(cotz[pl.ds(r0, 256), :], w2[x, :, cols], preferred_element_type=F32)
            dystored[pl.ds(r0, 256), :] = (val + dyrecv[c, pl.ds(r0, 256), :].astype(F32)).astype(BF16)
            return carry

        lax.fori_loop(0, L // 256, mine, 0)
        dypos[pl.ds(0, L), :] = jnp.dot(perm[...], dystored[...], preferred_element_type=F32)

        def backward(n, carry):
            h0 = pl.multiple_of(lax.rem(n, 2) * 128, 128)
            c0 = pl.multiple_of(c * 256 + h0, 128)
            r0 = pl.multiple_of((n // 2) * STRIP, STRIP)
            m = mask[pl.ds(r0 + 8, STRIP + 16), :]
            filt = [[short[pl.ds(t * 3 + a, 1), pl.ds(c0, 128)] for t in range(3)] for a in range(3)]
            h = [inner[pl.ds(t, 1), pl.ds(c0, 128)] for t in range(7)]
            us, feats = [], []
            for a in range(3):
                u = upos[pl.ds(r0, STRIP + 2 * PAD), pl.ds(a * CB + c0, 128)].astype(F32)[8 : STRIP + 24]
                f, u1, u2 = taps3(u, m, filt[a])
                us.append((u, u1, u2))
                feats.append(f)
            q, k, v = feats
            dy = dypos[pl.ds(r0, STRIP + 8), pl.ds(h0, 128)]
            dw = dy * q[8:]
            inside = STRIP // 8

            def total(val):
                return jnp.sum(val.reshape(inside, 8, 128), axis=0)

            zt = k * v
            w = h[0] * zt
            mb = m[8:]
            back = dw
            dz = h[0] * dw
            gacc[9, :, pl.ds(c0, 128)] += total(dw[:STRIP] * zt[8 : STRIP + 8])
            for t in range(1, 7):
                zt = down(zt, m)
                w = w + h[t] * zt
                gacc[9 + t, :, pl.ds(c0, 128)] += total(dw[:STRIP] * zt[8 : STRIP + 8])
                back = up(back, mb)
                dz = dz + h[t] * back
            df = (dy * w[8:], dz * v[8:], dz * k[8:])
            for a in range(3):
                for t in range(3):
                    gacc[t * 3 + a, :, pl.ds(c0, 128)] += total(df[a][:STRIP] * us[a][t][8 : STRIP + 8])
                b1 = up(df[a], mb)
                b2 = up(b1, mb)
                du = filt[a][0] * df[a] + filt[a][1] * b1 + filt[a][2] * b2
                dupos[pl.ds(r0, STRIP), pl.ds(a * 256 + h0, 128)] = du[:STRIP].astype(BF16)
            return carry

        lax.fori_loop(0, 2 * (L // STRIP), backward, 0)
        for a in range(3):
            cc = pl.ds(a * 256, 256)
            dusend[c, :, cc] = jnp.dot(permt[...], dupos[:, cc], preferred_element_type=F32).astype(BF16)
        for n, (dx, dz_) in enumerate(A2A):
            p = peer(x, z, dx, dz_)
            cp = pltpu.make_async_remote_copy(
                dusend.at[c, pl.ds(p * ROWS, ROWS)], dugot.at[c, j], q_s.at[c, n], q_r.at[c, n],
                device_id={"ctx": p}, device_id_type=MESH,
            )
            cp.start()
            d_a.append(cp)
        lc = pltpu.make_async_copy(dusend.at[c, pl.ds(j * ROWS, ROWS)], dugot.at[c, j], l_s.at[c])
        lc.start()
        d_a.append(lc)
        if c == 0:
            product(0, put_own)
            for cp in (t_u, t_d, f_u, f_d):
                cp.wait_recv()

            def finish(a, dst):
                def step(n, carry):
                    r0 = pl.multiple_of(n * 16, 16)
                    rs = pl.ds(r0, 16)
                    final[dst, rs, :] = (
                        own[a, rs, :] + (got2[0, a, rs, :].astype(F32) + got2[1, a, rs, :].astype(F32))
                    ).astype(BF16)
                    return carry

                lax.fori_loop(0, ROWS // 16, step, 0)

            finish(1 - x, 0)
            m_x = copy(final.at[0], mixed.at[:, pl.ds(x * HF, HF)], 6, xb)
            finish(x, 1)
            m_own = pltpu.make_async_copy(final.at[1], mixed.at[:, pl.ds(x * HF, HF)], l_s.at[2])
            m_own.start()

    for k in range(16):
        gall[0, pl.ds(k, 1), :] = jnp.sum(gacc[k], axis=0, keepdims=True)
    g_x = []
    for n in range(1, 16):
        cp = pltpu.make_async_remote_copy(
            gall.at[0], gall.at[n], g_s.at[n], g_r.at[n], device_id={"dp": dps[n - 1]}, device_id_type=MESH
        )
        cp.start()
        g_x.append(cp)
    for cp in g_x:
        cp.wait()
    total_g = gall[0]
    for n in range(1, 16):
        total_g = total_g + gall[n]
    grads[...] = total_g
    m_own.wait()
    m_x.wait()
    for cp in (s_u, s_d, t_u, t_d, f_u, f_d):
        cp.wait_send()
    for cp in d_x:
        cp.wait_send()
    for cp in d_a:
        cp.wait()


VM = pl.BlockSpec(memory_space=pltpu.VMEM)
SM = pl.BlockSpec(memory_space=pltpu.SMEM)
HB = pl.BlockSpec(memory_space=pl.ANY)
DMA = pltpu.SemaphoreType.DMA


def front(qs, cot, order_row, order_col, lens, short, inner):
    sds = jax.ShapeDtypeStruct
    return pl.pallas_call(
        front_kernel,
        out_shape=(sds((L + 2 * PAD, 3 * CB), BF16), sds((2, 4, ROWS, HF), BF16), sds((L, 2 * CB), BF16)),
        in_specs=[HB, HB, VM, VM, SM, VM, VM],
        out_specs=(VM, HB, HB),
        scratch_shapes=[
            pltpu.VMEM((L, 3 * CB), BF16),
            pltpu.VMEM((L, L), BF16),
            pltpu.VMEM((L + 2 * PAD, 128), F32),
            pltpu.VMEM((L, CB), BF16),
            pltpu.VMEM((L, CB), BF16),
            DMA((7,)), DMA((7,)), DMA((8,)), DMA((8,)), DMA((3,)),
        ],
        compiler_params=pltpu.CompilerParams(collective_id=0, has_side_effects=True, vmem_limit_bytes=40 << 20),
        cost_estimate=pl.CostEstimate(flops=10 << 30, bytes_accessed=200 << 20, transcendentals=0),
        name="front",
    )(qs, cot, order_row, order_col, lens, short, inner)


def back(cotz, y, w2, upos, order_row, order_col, lens, short, inner):
    sds = jax.ShapeDtypeStruct
    return pl.pallas_call(
        back_kernel,
        out_shape=(sds((ROWS, 2 * HF), BF16), sds((2, 8, ROWS, 768), BF16), sds((16, CB), F32)),
        in_specs=[VM, VM, VM, VM, VM, VM, SM, VM, VM],
        out_specs=(HB, HB, VM),
        scratch_shapes=[
            pltpu.VMEM((L, L), BF16),
            pltpu.VMEM((L, L), BF16),
            pltpu.VMEM((L + 2 * PAD, 128), F32),
            pltpu.VMEM((2, L, 256), BF16),
            pltpu.VMEM((2, L, 256), BF16),
            pltpu.VMEM((L, 256), BF16),
            pltpu.VMEM((L + 8, 256), F32),
            pltpu.VMEM((L, 768), BF16),
            pltpu.VMEM((2, L, 768), BF16),
            pltpu.VMEM((2 * ROWS, 2 * CB), BF16),
            pltpu.VMEM((2, ROWS, HF), F32),
            pltpu.VMEM((2, ROWS, HF), F32),
            pltpu.VMEM((2, ROWS, HF), BF16),
            pltpu.VMEM((2, ROWS, HF), BF16),
            pltpu.VMEM((2, ROWS, HF), BF16),
            pltpu.VMEM((2, ROWS, HF), BF16),
            pltpu.VMEM((2, 2, ROWS, HF), BF16),
            pltpu.VMEM((2, ROWS, HF), BF16),
            pltpu.VMEM((16, 8, CB), F32),
            pltpu.VMEM((16, 16, CB), F32),
            DMA((2,)), DMA((2,)), DMA((7,)), DMA((7,)), DMA((2, 7)), DMA((2, 7)), DMA((16,)), DMA((16,)), DMA((3,)),
        ],
        compiler_params=pltpu.CompilerParams(collective_id=1, has_side_effects=True, vmem_limit_bytes=58 << 20),
        cost_estimate=pl.CostEstimate(flops=20 << 30, bytes_accessed=250 << 20, transcendentals=0),
        name="back",
    )(cotz, y, w2, upos, order_row, order_col, lens, short, inner)


def swap_pairs():
    pairs = []
    for hi in range(2):
        for yc in range(8):
            for lo in range(2):
                for z in range(4):
                    pairs.append((((hi * 8 + yc) * 8 + lo * 4 + z), ((lo * 8 + yc) * 8 + hi * 4 + z)))
    return pairs


def on_device(qkv, short_filter, inner_filter, out_weight, cotangent, order, lengths):
    pairs = swap_pairs()
    swapped = lax.ppermute(out_weight, ("dp", "ctx"), pairs)
    w2 = lax.all_gather(swapped, "dp", axis=0, tiled=True).reshape(2, HF, CB)
    qs = qkv.reshape(ROWS, 3, 8, CB).transpose(2, 0, 1, 3).reshape(8, ROWS, 3 * CB)
    short = short_filter.reshape(9, CB)
    inner = jnp.repeat(inner_filter, GROUP, axis=1)
    order_col = order.reshape(L, 1)
    upos, cotz, y = front(qs, cotangent, order, order_col, lengths, short, inner)
    cotz = cotz.reshape(L, HF)
    gw = lax.dot_general(
        jnp.stack([y[:, :CB], y[:, CB:]]), cotz, (((1,), (0,)), ((), ())), preferred_element_type=F32
    )
    gw = gw.transpose(0, 2, 1).astype(BF16).reshape(2 * HF, CB)
    gw = lax.psum_scatter(gw, "dp", scatter_dimension=0, tiled=True)
    gw = lax.ppermute(gw, ("dp", "ctx"), pairs).astype(F32)
    mixed, dugot, grads = back(cotz, y, w2, upos, order, order_col, lengths, short, inner)
    grad_qkv = dugot.reshape(2, 8, ROWS, 3, 256).transpose(2, 3, 1, 0, 4).reshape(ROWS, 3, 8 * CB)
    grad_short = grads[:9].reshape(3, 3, CB)
    grad_inner = grads[9:].reshape(7, CB // GROUP, GROUP).sum(-1)
    return (mixed, grad_qkv, gw, grad_short, grad_inner)


def solution(mesh):
    in_specs = (
        P(("dp", "ctx"), None, None),
        P(None, None, "ctx"),
        P(None, "ctx"),
        P("dp", "ctx"),
        P(("dp", "ctx"), None),
        P("dp", None),
        P("dp", None),
    )
    out_specs = (
        P(("dp", "ctx"), None),
        P(("dp", "ctx"), None, None),
        P("dp", "ctx"),
        P(None, None, "ctx"),
        P(None, "ctx"),
    )
    return jax.shard_map(on_device, mesh=mesh, in_specs=in_specs, out_specs=out_specs, check_vma=False)
```

```python
import jax
import jax.numpy as jnp
from jax import lax
from jax.sharding import PartitionSpec as P
from jax.experimental import pallas as pl
from jax.experimental.pallas import tpu as pltpu

MESH = pl.DeviceIdType.MESH
F32 = jnp.float32
BF16 = jnp.bfloat16
GROUP = 16
L = 1024
CB = 512
HF = 2048
ROWS = 128
PAD = 16
STRIP = 128
A2A = ((0, 2), (1, 2), (1, 1), (1, 3), (0, 1), (0, 3), (1, 0))


def where_am_i():
    j = lax.axis_index("ctx")
    return j, j // 4, lax.rem(j, 4)


def peer(x, z, dx, dz):
    return lax.rem(x + dx, 2) * 4 + lax.rem(z + dz, 4)


def barrier(ids):
    sem = pltpu.get_barrier_semaphore()
    for d in ids:
        pl.semaphore_signal(sem, inc=1, device_id=d, device_id_type=MESH)
    pl.semaphore_wait(sem, len(ids))


def fill_masks(lens_ref, m_ref):
    p = lax.broadcasted_iota(jnp.int32, m_ref.shape, 0) - PAD
    good = (p > 0) & (p < L)
    end = jnp.int32(0)
    for k in range(lens_ref.shape[1]):
        end = end + lens_ref[0, k]
        good = good & (p != end)
    m_ref[...] = jnp.where(good, 1.0, 0.0).astype(F32)


def fill_gather(order_row_ref, out_ref):
    def step(i, c):
        r0 = pl.multiple_of(i * 128, 128)
        p = lax.broadcasted_iota(jnp.int32, (128, L), 0) + r0
        out_ref[pl.ds(r0, 128), :] = jnp.where(p == order_row_ref[...], 1.0, 0.0).astype(BF16)
        return c

    lax.fori_loop(0, L // 128, step, 0)


def down(x, m):
    return pltpu.roll(x, 1, 0) * m


def up(x, m):
    return pltpu.roll(x * m, x.shape[0] - 1, 0)


def taps3(u, m, filt):
    u1 = down(u, m)
    u2 = down(u1, m)
    return filt[0] * u + filt[1] * u1 + filt[2] * u2


def dp_id(h, yy, c):
    return h * 8 + yy * 2 + c


def coords():
    i = lax.axis_index("dp")
    return i, i // 8, lax.rem(i // 2, 4), lax.rem(i, 2)


def strips(rows, step, fn):
    def body(n, carry):
        fn(pl.ds(pl.multiple_of(n * step, step), step))
        return carry

    lax.fori_loop(0, rows // step, body, 0)


def block_kernel(
    qs, cot, wt, order_row, lens, short, inner_g,
    mixed, dugot, gw_out, short_out, inner_out,
    arrived, upos, feats, perm, mask, ypos, y, cotz, w2, inner,
    dysend, dyrecv, dypos, dupos,
    parts, fwd, got1, got2, final, gacc, gall,
    gsib, ggot, gown, gfwd, ggot1, ggot2, gred, gfin,
    a_s, a_r, c_s, c_r, w_s, w_r, r_s, r_r, q_s, q_r, g_s, g_r, v_s, v_r, l_s,
):
    j, x, z = where_am_i()
    i, h, yy, core = coords()
    xb = peer(x, z, 1, 0)
    zul, zdl, zo = lax.rem(z + 1, 4), lax.rem(z + 3, 4), lax.rem(z + 2, 4)
    zu, zd = x * 4 + zul, x * 4 + zdl
    yu, yd, yo = lax.rem(yy + 1, 4), lax.rem(yy + 3, 4), lax.rem(yy + 2, 4)
    up_y, dn_y, sib = dp_id(h, yu, core), dp_id(h, yd, core), dp_id(h, yy, 1 - core)
    over_y, flip = dp_id(h, yo, core), dp_id(1 - h, yy, core)
    barrier(
        [{"ctx": peer(x, z, dx, dz)} for dx, dz in A2A]
        + [{"dp": up_y}, {"dp": dn_y}, {"dp": over_y}, {"dp": sib}, {"dp": flip}]
        + [{"dp": flip, "ctx": xb}]
    )

    def remote(src, dst, sems, n, to, rn=None):
        return pltpu.make_async_remote_copy(
            src, dst, sems[0].at[n], sems[1].at[n if rn is None else rn], device_id=to, device_id_type=MESH
        )

    def send(src, dst, sems, n, to, rn=None):
        c = remote(src, dst, sems, n, to, rn)
        c.start()
        return c

    def cols(k, width):
        return pl.ds(pl.multiple_of(k * width, width), width)

    mine_rows = pl.ds(pl.multiple_of(j * ROWS, ROWS), ROWS)
    a_in = []
    for n, (dx, dz) in enumerate(A2A):
        p = peer(x, z, dx, dz)
        a_in.append(send(qs.at[:, :, cols(p, CB)], arrived.at[:, mine_rows, :], (a_s, a_r), n, {"ctx": p}))
    own_q = pltpu.make_async_copy(qs.at[:, :, cols(j, CB)], arrived.at[:, mine_rows, :], l_s.at[0])
    own_q.start()

    wsem = (w_s, w_r)
    w_mine = w2.at[x, yy * 2 + core]
    w_a = send(wt, w_mine, wsem, 0, {"dp": flip, "ctx": h * 4 + z}, x)
    w_b = remote(wt, w_mine, wsem, 1, {"ctx": h * 4 + z}, x)
    w_l = pltpu.make_async_copy(wt, w_mine, l_s.at[3])

    @pl.when(h != x)
    def _():
        w_b.start()

    @pl.when(h == x)
    def _():
        w_l.start()

    mine_c = cot.at[:, cols(x, HF)]
    own_c = pltpu.make_async_copy(mine_c, cotz.at[x, z], l_s.at[1])
    own_c.start()

    fill_masks(lens, mask)
    fill_gather(order_row, perm)
    upos[pl.ds(0, PAD), :] = jnp.zeros((PAD, 3 * CB), BF16)
    upos[pl.ds(PAD + L, PAD), :] = jnp.zeros((PAD, 3 * CB), BF16)
    feats[:, pl.ds(L, PAD), :] = jnp.zeros((4, PAD, CB), BF16)
    gacc[...] = jnp.zeros_like(gacc)
    dypos[pl.ds(L, 8), :] = jnp.zeros((8, CB), F32)
    group_of = lax.broadcasted_iota(jnp.int32, (CB // GROUP, CB), 1) // GROUP
    spread = jnp.where(group_of == lax.broadcasted_iota(jnp.int32, (CB // GROUP, CB), 0), 1.0, 0.0).astype(F32)
    inner[...] = jnp.dot(inner_g[...], spread, preferred_element_type=F32, precision=lax.Precision.HIGHEST)

    remote(wt, w2.at[1 - x, yy * 2 + core], wsem, 0, {"ctx": xb}, 1 - x).wait_recv()

    @pl.when(h != x)
    def _():
        remote(wt, w_mine, wsem, 0, {"ctx": xb}, x).wait_recv()

    @pl.when(h == x)
    def _():
        w_l.wait()

    def pair(k):
        return w2.at[:, k * 2 + core]

    def again(ref, n, to):
        return send(ref, ref, wsem, n, {"dp": to})

    wy = [again(pair(yy), 2, up_y), again(pair(yy), 3, dn_y)]
    ws = [again(pair(yy), 6, sib)]
    wy[0].wait_recv()
    wy[1].wait_recv()
    wy += [again(w2.at[0, yd * 2 + core], 4, up_y), again(w2.at[1, yu * 2 + core], 5, dn_y)]
    ws += [again(pair(yd), 7, sib), again(pair(yu), 8, sib)]

    own_q.wait()
    for c in a_in:
        c.wait_recv()

    csem = (c_s, c_r)
    over = send(cot.at[:, cols(1 - x, HF)], cotz.at[x, z], csem, 0, {"ctx": xb})
    u_own = send(mine_c, cotz.at[x, z], csem, 1, {"ctx": zu})
    d_own = send(mine_c, cotz.at[x, z], csem, 2, {"ctx": zd})

    def place(a, c):
        upos[pl.ds(PAD, L), cols(a, CB)] = jnp.dot(perm[...], arrived[a], preferred_element_type=F32).astype(BF16)
        return c

    lax.fori_loop(0, 3, place, 0)

    over.wait_recv()
    theirs = cotz.at[1 - x, z]
    u_oth = send(theirs, theirs, csem, 3, {"ctx": zu})
    d_oth = send(theirs, theirs, csem, 4, {"ctx": zd})

    def forward(n, carry):
        c0 = pl.multiple_of(lax.rem(n, CB // 128) * 128, 128)
        cs = pl.ds(c0, 128)
        r0 = pl.multiple_of((n // (CB // 128)) * STRIP, STRIP)
        m = mask[pl.ds(r0 + 8, STRIP + 8), :]
        made = []
        for a in range(3):
            u = upos[pl.ds(r0, STRIP + PAD), pl.ds(a * CB + c0, 128)].astype(F32)[8:]
            made.append(taps3(u, m, [short[t, pl.ds(a, 1), cs] for t in range(3)]))
        q, k, v = made
        zt = k * v
        w = inner[pl.ds(0, 1), cs] * zt
        for t in range(1, 7):
            zt = down(zt, m)
            w = w + inner[pl.ds(t, 1), cs] * zt
        for a, val in enumerate((q, k, v, w)):
            feats[a, pl.ds(r0, STRIP), cs] = val[8:].astype(BF16)
        ypos[pl.ds(r0, STRIP), cs] = (q * w)[8:].astype(BF16)
        return carry

    lax.fori_loop(0, (CB // 128) * (L // STRIP), forward, 0)
    my_y = cols(x, CB)
    y[:, my_y] = lax.dot_general(perm[...], ypos[...], TN, preferred_element_type=F32).astype(BF16)
    y_x = send(y.at[:, my_y], y.at[:, my_y], csem, 7, {"ctx": xb})

    wy[2].wait_recv()
    wy[3].wait_recv()
    ws.append(again(pair(yo), 9, sib))
    for c in ws:
        c.wait_recv()
    own_c.wait()

    def grads_of(zz):
        lhs = cotz[:, zz].reshape(2 * ROWS, HF)
        there = jnp.dot(lhs, w2[1 - x].reshape(HF, CB), preferred_element_type=F32).astype(BF16)
        here = jnp.dot(lhs, w2[x].reshape(HF, CB), preferred_element_type=F32)
        for a in range(2):
            rs = pl.ds(pl.multiple_of(a * 512 + zz * ROWS, ROWS), ROWS)
            dysend[rs, :] = there[a * ROWS : (a + 1) * ROWS]
            dypos[rs, :] = here[a * ROWS : (a + 1) * ROWS]

    def grads_step(n, carry):
        grads_of(lax.rem(z + 1 + 2 * n, 4))
        return carry

    grads_of(z)
    u_own.wait_recv()
    d_own.wait_recv()
    u_oth.wait_recv()
    d_oth.wait_recv()
    on_u = send(cotz.at[0, zdl], cotz.at[0, zdl], csem, 5, {"ctx": zu})
    on_d = send(cotz.at[1, zul], cotz.at[1, zul], csem, 6, {"ctx": zd})
    lax.fori_loop(0, 2, grads_step, 0)
    on_u.wait_recv()
    on_d.wait_recv()
    grads_of(zo)
    d_x = send(dysend, dyrecv, csem, 8, {"ctx": xb})

    y_x.wait_recv()

    def part(n, carry):
        def rows_of(b):
            return w2[b, pl.ds(n * 2, 2)].reshape(512, CB)

        val = lax.dot_general(y[:, pl.ds(0, CB)], rows_of(0), NT, preferred_element_type=F32) + lax.dot_general(
            y[:, pl.ds(CB, CB)], rows_of(1), NT, preferred_element_type=F32
        )
        for a in range(2):
            for zz in range(4):
                r0 = (a * 4 + zz) * ROWS
                parts[lax.rem(zz - z + 4, 4), a, :, cols(n, 512)] = val[r0 : r0 + ROWS].astype(BF16)
        return carry

    lax.fori_loop(0, HF // 512, part, 0)
    rsem = (r_s, r_r)
    s_u = send(parts.at[2, 0], got1.at[0], rsem, 0, {"ctx": zu})
    s_d = send(parts.at[2, 1], got1.at[1], rsem, 1, {"ctx": zd})

    vsem = (v_s, v_r)

    def weights(which, dst):
        def step(k, carry):
            lhs = cotz[:, :, :, cols(k * 2 + which, 256)].reshape(L, 256)
            val = lax.dot_general(lhs, y[...], TN, preferred_element_type=F32).astype(BF16)
            dst[k, 0] = val[:, :CB]
            dst[k, 1] = val[:, CB:]
            return carry

        lax.fori_loop(0, 4, step, 0)

    weights(1 - core, gsib)
    g_sib = send(gsib, ggot, vsem, 0, {"dp": sib})
    t_u = send(parts.at[1, 1], got2.at[0, 1], rsem, 2, {"ctx": zu})
    t_d = send(parts.at[3, 0], got2.at[1, 0], rsem, 3, {"ctx": zd})
    weights(core, gown)

    def combine(a, k):
        def fn(rs):
            fwd[a, rs, :] = (parts[k, a, rs, :].astype(F32) + got1[a, rs, :].astype(F32)).astype(BF16)

        strips(ROWS, 16, fn)

    s_u.wait_recv()
    combine(0, 1)
    f_u = send(fwd.at[0], got2.at[0, 0], rsem, 4, {"ctx": zu})
    s_d.wait_recv()
    combine(1, 3)
    f_d = send(fwd.at[1], got2.at[1, 1], rsem, 5, {"ctx": zd})

    g_sib.wait_recv()

    def add_pairs(n, carry):
        k, b = n // 2, lax.rem(n, 2)

        def fn(rs):
            gown[k, b, rs, :] = (gown[k, b, rs, :].astype(F32) + ggot[k, b, rs, :].astype(F32)).astype(BF16)

        strips(256, 64, fn)
        return carry

    lax.fori_loop(0, 8, add_pairs, 0)
    gy = [
        send(gown.at[yo, 0], ggot1.at[0], vsem, 1, {"dp": up_y}),
        send(gown.at[yo, 1], ggot1.at[1], vsem, 2, {"dp": dn_y}),
        send(gown.at[yu, 1], ggot2.at[0, 1], vsem, 3, {"dp": up_y}),
        send(gown.at[yd, 0], ggot2.at[1, 0], vsem, 4, {"dp": dn_y}),
    ]

    d_x.wait_recv()

    def add_dy(rs):
        ypos[rs, :] = (dypos[rs, :] + dyrecv[rs, :].astype(F32)).astype(BF16)

    strips(L, 64, add_dy)
    dypos[pl.ds(0, L), :] = jnp.dot(perm[...], ypos[...], preferred_element_type=F32)

    a_out = []
    for c in range(2):

        def backward(n, carry):
            h0 = pl.multiple_of(lax.rem(n, 2) * 128, 128)
            cs = pl.ds(pl.multiple_of(c * 256 + h0, 128), 128)
            r0 = pl.multiple_of((n // 2) * STRIP, STRIP)
            m = mask[pl.ds(r0 + PAD, STRIP + 8), :]
            q, k, v, w = [feats[a, pl.ds(r0, STRIP + PAD), cs].astype(F32)[: STRIP + 8] for a in range(4)]
            dy = dypos[pl.ds(r0, STRIP + 8), cs]

            def total(val):
                return jnp.sum(val.reshape(STRIP // 8, 8, 128), axis=0)

            b = dy * q
            zs = (k * v)[:STRIP]
            dz = inner[pl.ds(0, 1), cs] * b
            gacc[9, :, cs] += total(b[:STRIP] * zs)
            for t in range(1, 7):
                b = up(b, m)
                dz = dz + inner[pl.ds(t, 1), cs] * b
                gacc[9 + t, :, cs] += total(b[:STRIP] * zs)
            df = (dy * w, dz * v, dz * k)
            for a in range(3):
                u = upos[pl.ds(PAD + r0, STRIP), pl.ds(pl.multiple_of(a * CB + c * 256 + h0, 128), 128)].astype(F32)
                b = df[a]
                du = short[0, pl.ds(a, 1), cs] * b
                gacc[a, :, cs] += total(b[:STRIP] * u)
                for t in range(1, 3):
                    b = up(b, m)
                    du = du + short[t, pl.ds(a, 1), cs] * b
                    gacc[t * 3 + a, :, cs] += total(b[:STRIP] * u)
                dupos[pl.ds(r0, STRIP), pl.ds(pl.multiple_of(a * 256 + h0, 128), 128)] = du[:STRIP].astype(BF16)
            return carry

        lax.fori_loop(0, 2 * (L // STRIP), backward, 0)
        val = lax.dot_general(perm[...], dupos[...], TN, preferred_element_type=F32).astype(BF16)
        part_c = pl.ds(c * 256, 256)
        for a in range(3):
            arrived[a, :, part_c] = val[:, a * 256 : (a + 1) * 256]
        there = dugot.at[:, :, pl.ds(pl.multiple_of(j * CB + c * 256, 256), 256)]
        for n, (dx, dz_) in enumerate(A2A):
            p = peer(x, z, dx, dz_)
            rs = pl.ds(pl.multiple_of(p * ROWS, ROWS), ROWS)
            a_out.append(send(arrived.at[:, rs, part_c], there, (q_s, q_r), c * 7 + n, {"ctx": p}))
        lc = pltpu.make_async_copy(arrived.at[:, mine_rows, part_c], there, l_s.at[4 + c])
        lc.start()
        a_out.append(lc)
        if c == 0:
            gy[0].wait_recv()
            gy[1].wait_recv()
            for a, k in ((0, yu), (1, yd)):

                def add_fwd(rs):
                    gfwd[a, rs, :] = (gown[k, a, rs, :].astype(F32) + ggot1[a, rs, :].astype(F32)).astype(BF16)

                strips(256, 64, add_fwd)
            gy.append(send(gfwd.at[0], ggot2.at[0, 0], vsem, 5, {"dp": up_y}))
            gy.append(send(gfwd.at[1], ggot2.at[1, 1], vsem, 6, {"dp": dn_y}))

    for k in range(16):
        gall[0, pl.ds(k, 1), :] = jnp.sum(gacc[k], axis=0, keepdims=True)
    near_y = dp_id(h, yy + 1 - 2 * lax.rem(yy, 2), core)
    gx = []

    def exchange(n):
        gx.append(send(gall.at[2 * n], gall.at[2 * n + 1], (g_s, g_r), n, {"dp": (sib, near_y, over_y, flip)[n]}))

    def summed(n):
        gx[n].wait_recv()
        gall[2 * n + 2] = gall[2 * n] + gall[2 * n + 1]

    exchange(0)

    for cp in (t_u, t_d, f_u, f_d):
        cp.wait_recv()

    def finish(a, dst):
        def fn(rs):
            final[dst, rs, :] = (
                parts[0, a, rs, :].astype(F32) + (got2[0, a, rs, :].astype(F32) + got2[1, a, rs, :].astype(F32))
            ).astype(BF16)

        strips(ROWS, 16, fn)

    finish(1 - x, 0)
    m_x = send(final.at[0], mixed.at[:, cols(x, HF)], rsem, 6, {"ctx": xb})
    summed(0)
    exchange(1)
    finish(x, 1)
    m_own = pltpu.make_async_copy(final.at[1], mixed.at[:, cols(x, HF)], l_s.at[2])
    m_own.start()

    for k in range(2, 6):
        gy[k].wait_recv()
    for a in range(2):

        def add_all(rs):
            gred[a, rs, :] = (
                gown[yy, a, rs, :].astype(F32) + (ggot2[0, a, rs, :].astype(F32) + ggot2[1, a, rs, :].astype(F32))
            ).astype(BF16)

        strips(256, 64, add_all)

    def owner_copy(a):
        return remote(gred.at[a], gfin.at[h], vsem, 7 + a, {"dp": dp_id(x, yy, core), "ctx": a * 4 + z}, 7 + h)

    for a in range(2):

        @pl.when((h != x) | (x != a))
        def _():
            owner_copy(a).start()

    @pl.when(h == x)
    def _():
        def keep(rs):
            gfin[h, rs, :] = gred[x, rs, :]

        strips(256, 64, keep)

    summed(1)
    exchange(2)
    summed(2)
    exchange(3)
    summed(3)
    sums = gall[8]
    for t in range(3):
        short_out[t] = sums[t * 3 : t * 3 + 3]
    inner_out[...] = lax.dot_general(
        sums[9:16], spread, NT, preferred_element_type=F32, precision=lax.Precision.HIGHEST
    )

    for s in range(2):

        @pl.when((h != x) | (h != s))
        def _():
            remote(gred.at[0], gfin.at[s], vsem, 7, {"ctx": xb}, 7 + s).wait_recv()

    def last(rs):
        gw_out[rs, :] = gfin[0, rs, :].astype(F32) + gfin[1, rs, :].astype(F32)

    strips(256, 64, last)

    for a in range(2):

        @pl.when((h != x) | (x != a))
        def _():
            owner_copy(a).wait_send()

    @pl.when(h != x)
    def _():
        w_b.wait_send()

    m_own.wait()
    m_x.wait()
    for cp in (w_a, *wy, *ws, *a_in, over, u_own, d_own, u_oth, d_oth, on_u, on_d, y_x, d_x):
        cp.wait_send()
    for cp in (s_u, s_d, t_u, t_d, f_u, f_d, g_sib, *gy, *gx):
        cp.wait_send()
    for cp in a_out:
        cp.wait()


VM = pl.BlockSpec(memory_space=pltpu.VMEM)
SM = pl.BlockSpec(memory_space=pltpu.SMEM)
HB = pl.BlockSpec(memory_space=pl.ANY)
DMA = pltpu.SemaphoreType.DMA
NT = (((1,), (1,)), ((), ()))
TN = (((0,), (0,)), ((), ()))


def sems(*counts):
    return [DMA((n,)) for n in counts for _ in range(2)]


def block(qs, cot, wt, order_row, lens, short, inner):
    sds = jax.ShapeDtypeStruct
    vm = pltpu.VMEM
    return pl.pallas_call(
        block_kernel,
        out_shape=(
            sds((ROWS, 2 * HF), BF16),
            sds((3, ROWS, 8 * CB), BF16),
            sds((256, CB), F32),
            sds((3, 3, CB), F32),
            sds((7, CB // GROUP), F32),
        ),
        in_specs=[HB, HB, HB, VM, SM, VM, VM],
        out_specs=(HB, HB, VM, VM, VM),
        scratch_shapes=[
            vm((3, L, CB), BF16),
            vm((L + 2 * PAD, 3 * CB), BF16),
            vm((4, L + PAD, CB), BF16),
            vm((L, L), BF16),
            vm((L + 2 * PAD, 128), F32),
            vm((L, CB), BF16),
            vm((L, 2 * CB), BF16),
            vm((2, 4, ROWS, HF), BF16),
            vm((2, 8, 256, CB), BF16),
            vm((7, CB), F32),
            vm((L, CB), BF16),
            vm((L, CB), BF16),
            vm((L + 8, CB), F32),
            vm((L, 768), BF16),
            vm((4, 2, ROWS, HF), BF16),
            vm((2, ROWS, HF), BF16),
            vm((2, ROWS, HF), BF16),
            vm((2, 2, ROWS, HF), BF16),
            vm((2, ROWS, HF), BF16),
            vm((16, 8, CB), F32),
            vm((9, 16, CB), F32),
            vm((4, 2, 256, CB), BF16),
            vm((4, 2, 256, CB), BF16),
            vm((4, 2, 256, CB), BF16),
            vm((2, 256, CB), BF16),
            vm((2, 256, CB), BF16),
            vm((2, 2, 256, CB), BF16),
            vm((2, 256, CB), BF16),
            vm((2, 256, CB), BF16),
            *sems(7, 9, 10, 7, 14, 4, 9),
            DMA((6,)),
        ],
        compiler_params=pltpu.CompilerParams(collective_id=0, has_side_effects=True, vmem_limit_bytes=60 << 20),
        cost_estimate=pl.CostEstimate(flops=30 << 30, bytes_accessed=100 << 20, transcendentals=0),
        name="block",
    )(qs, cot, wt, order_row, lens, short, inner)


def on_device(qkv, short_filter, inner_filter, out_weight, cotangent, order, lengths):
    qs = qkv.transpose(1, 0, 2)
    mixed, dugot, gw, grad_short, grad_inner = block(
        qs, cotangent, out_weight, order, lengths, short_filter, inner_filter
    )
    return (mixed, dugot.transpose(1, 0, 2), gw, grad_short, grad_inner)


def solution(mesh):
    in_specs = (
        P(("dp", "ctx"), None, None),
        P(None, None, "ctx"),
        P(None, "ctx"),
        P("dp", "ctx"),
        P(("dp", "ctx"), None),
        P("dp", None),
        P("dp", None),
    )
    out_specs = (
        P(("dp", "ctx"), None),
        P(("dp", "ctx"), None, None),
        P("dp", "ctx"),
        P(None, None, "ctx"),
        P(None, "ctx"),
    )
    return jax.shard_map(on_device, mesh=mesh, in_specs=in_specs, out_specs=out_specs, check_vma=False)
```

```python
import jax
import jax.numpy as jnp
from jax import lax
from jax.sharding import PartitionSpec as P
from jax.experimental import pallas as pl
from jax.experimental.pallas import tpu as pltpu

MESH = pl.DeviceIdType.MESH
F32 = jnp.float32
BF16 = jnp.bfloat16
GROUP = 16
L = 1024
CB = 512
HF = 2048
ROWS = 128
PAD = 16
STRIP = 128
A2A = ((0, 2), (1, 2), (1, 1), (1, 3), (0, 1), (0, 3), (1, 0))


def where_am_i():
    j = lax.axis_index("ctx")
    return j, j // 4, lax.rem(j, 4)


def peer(x, z, dx, dz):
    return lax.rem(x + dx, 2) * 4 + lax.rem(z + dz, 4)


def barrier(ids):
    sem = pltpu.get_barrier_semaphore()
    for d in ids:
        pl.semaphore_signal(sem, inc=1, device_id=d, device_id_type=MESH)
    pl.semaphore_wait(sem, len(ids))


def fill_masks(lens_ref, m_ref):
    p = lax.broadcasted_iota(jnp.int32, m_ref.shape, 0) - PAD
    good = (p > 0) & (p < L)
    end = jnp.int32(0)
    for k in range(lens_ref.shape[1]):
        end = end + lens_ref[0, k]
        good = good & (p != end)
    m_ref[...] = jnp.where(good, 1.0, 0.0).astype(F32)


def fill_gather(order_row_ref, out_ref):
    def step(i, c):
        r0 = pl.multiple_of(i * 128, 128)
        p = lax.broadcasted_iota(jnp.int32, (128, L), 0) + r0
        out_ref[pl.ds(r0, 128), :] = jnp.where(p == order_row_ref[...], 1.0, 0.0).astype(BF16)
        return c

    lax.fori_loop(0, L // 128, step, 0)


def down(x, m):
    return pltpu.roll(x, 1, 0) * m


def up(x, m):
    return pltpu.roll(x * m, x.shape[0] - 1, 0)


def taps3(u, m, filt):
    u1 = down(u, m)
    u2 = down(u1, m)
    return filt[0] * u + filt[1] * u1 + filt[2] * u2


def dp_id(h, yy, c):
    return h * 8 + yy * 2 + c


def coords():
    i = lax.axis_index("dp")
    return i, i // 8, lax.rem(i // 2, 4), lax.rem(i, 2)


def strips(rows, step, fn):
    def body(n, carry):
        fn(pl.ds(pl.multiple_of(n * step, step), step))
        return carry

    lax.fori_loop(0, rows // step, body, 0)


def block_kernel(
    qs, cot, wt, order_row, lens, short, inner_g,
    mixed, dugot, gw_out, short_out, inner_out,
    arrived, upos, feats, perm, mask, ypos, y, cotz, w2, inner,
    dysend, dyrecv, dypos, dupos,
    parts, fwd, got1, got2, final, gacc, gall,
    gsib, ggot, gown, gfwd, ggot1, ggot2, gred, gfin,
    a_s, a_r, c_s, c_r, w_s, w_r, r_s, r_r, q_s, q_r, g_s, g_r, v_s, v_r, d_s, d_r, l_s,
):
    j, x, z = where_am_i()
    i, h, yy, core = coords()
    xb = peer(x, z, 1, 0)
    zul, zdl, zo = lax.rem(z + 1, 4), lax.rem(z + 3, 4), lax.rem(z + 2, 4)
    zu, zd = x * 4 + zul, x * 4 + zdl
    yu, yd, yo = lax.rem(yy + 1, 4), lax.rem(yy + 3, 4), lax.rem(yy + 2, 4)
    up_y, dn_y, sib = dp_id(h, yu, core), dp_id(h, yd, core), dp_id(h, yy, 1 - core)
    over_y, flip = dp_id(h, yo, core), dp_id(1 - h, yy, core)
    barrier(
        [{"ctx": peer(x, z, dx, dz)} for dx, dz in A2A]
        + [{"dp": up_y}, {"dp": dn_y}, {"dp": over_y}, {"dp": sib}, {"dp": flip}]
        + [{"dp": flip, "ctx": xb}]
    )

    def remote(src, dst, sems, n, to, rn=None):
        return pltpu.make_async_remote_copy(
            src, dst, sems[0].at[n], sems[1].at[n if rn is None else rn], device_id=to, device_id_type=MESH
        )

    def send(src, dst, sems, n, to, rn=None):
        c = remote(src, dst, sems, n, to, rn)
        c.start()
        return c

    def cols(k, width):
        return pl.ds(pl.multiple_of(k * width, width), width)

    wsem = (w_s, w_r)
    w_mine = w2.at[x, yy * 2 + core]
    w_a = send(wt, w_mine, wsem, 0, {"dp": flip, "ctx": h * 4 + z}, x)
    w_b = remote(wt, w_mine, wsem, 1, {"ctx": h * 4 + z}, x)
    w_l = pltpu.make_async_copy(wt, w_mine, l_s.at[3])

    @pl.when(h != x)
    def _():
        w_b.start()

    @pl.when(h == x)
    def _():
        w_l.start()

    mine_rows = pl.ds(pl.multiple_of(j * ROWS, ROWS), ROWS)

    def streams_in(half):
        made = []
        here = arrived.at[:, mine_rows, pl.ds(half * 256, 256)]

        def block_of(p):
            return qs.at[:, :, pl.ds(pl.multiple_of(p * CB + half * 256, 256), 256)]

        for n, (dx, dz) in enumerate(A2A):
            p = peer(x, z, dx, dz)
            made.append(send(block_of(p), here, (a_s, a_r), half * 7 + n, {"ctx": p}))
        own = pltpu.make_async_copy(block_of(j), here, l_s.at[(0, 8)[half]])
        own.start()
        return made, own

    a_in, own_q = streams_in(0)
    mine_c = cot.at[:, cols(x, HF)]
    own_c = pltpu.make_async_copy(mine_c, cotz.at[x, z], l_s.at[1])
    own_c.start()

    fill_masks(lens, mask)
    fill_gather(order_row, perm)
    upos[pl.ds(0, PAD), :] = jnp.zeros((PAD, 3 * CB), BF16)
    upos[pl.ds(PAD + L, PAD), :] = jnp.zeros((PAD, 3 * CB), BF16)
    feats[:, pl.ds(L, PAD), :] = jnp.zeros((4, PAD, CB), BF16)
    gacc[...] = jnp.zeros_like(gacc)
    dypos[pl.ds(L, 8), :] = jnp.zeros((8, CB), F32)
    group_of = lax.broadcasted_iota(jnp.int32, (CB // GROUP, CB), 1) // GROUP
    spread = jnp.where(group_of == lax.broadcasted_iota(jnp.int32, (CB // GROUP, CB), 0), 1.0, 0.0).astype(F32)
    inner[...] = jnp.dot(inner_g[...], spread, preferred_element_type=F32, precision=lax.Precision.HIGHEST)

    remote(wt, w2.at[1 - x, yy * 2 + core], wsem, 0, {"ctx": xb}, 1 - x).wait_recv()

    @pl.when(h != x)
    def _():
        remote(wt, w_mine, wsem, 0, {"ctx": xb}, x).wait_recv()

    @pl.when(h == x)
    def _():
        w_l.wait()

    def pair(k):
        return w2.at[:, k * 2 + core]

    def again(ref, n, to):
        return send(ref, ref, wsem, n, {"dp": to})

    wy = [again(pair(yy), 2, up_y), again(pair(yy), 3, dn_y)]
    ws = [again(pair(yy), 6, sib)]
    later, later_q = streams_in(1)

    def filters(half):
        def place(a, c):
            upos[pl.ds(PAD, L), pl.ds(pl.multiple_of(a * CB + half * 256, 256), 256)] = jnp.dot(
                perm[...], arrived[a, :, pl.ds(half * 256, 256)], preferred_element_type=F32
            ).astype(BF16)
            return c

        lax.fori_loop(0, 3, place, 0)

        def forward(n, carry):
            c0 = pl.multiple_of(half * 256 + lax.rem(n, 2) * 128, 128)
            cs = pl.ds(c0, 128)
            r0 = pl.multiple_of((n // 2) * STRIP, STRIP)
            m = mask[pl.ds(r0 + 8, STRIP + 8), :]
            made = []
            for a in range(3):
                u = upos[pl.ds(r0, STRIP + PAD), pl.ds(a * CB + c0, 128)].astype(F32)[8:]
                made.append(taps3(u, m, [short[t, pl.ds(a, 1), cs] for t in range(3)]))
            q, k, v = made
            zt = k * v
            w = inner[pl.ds(0, 1), cs] * zt
            for t in range(1, 7):
                zt = down(zt, m)
                w = w + inner[pl.ds(t, 1), cs] * zt
            for a, val in enumerate((q, k, v, w)):
                feats[a, pl.ds(r0, STRIP), cs] = val[8:].astype(BF16)
            ypos[pl.ds(r0, STRIP), cs] = (q * w)[8:].astype(BF16)
            return carry

        lax.fori_loop(0, 2 * (L // STRIP), forward, 0)
        my_y = pl.ds(pl.multiple_of(x * CB + half * 256, 256), 256)
        y[:, my_y] = lax.dot_general(
            perm[...], ypos[:, pl.ds(half * 256, 256)], TN, preferred_element_type=F32
        ).astype(BF16)
        return send(y.at[:, my_y], y.at[:, my_y], csem, 7 + half, {"ctx": xb})

    csem = (c_s, c_r)
    own_q.wait()
    for c in a_in:
        c.wait_recv()
    y_x = [filters(0)]

    wy[0].wait_recv()
    wy[1].wait_recv()
    wy += [again(w2.at[0, yd * 2 + core], 4, up_y), again(w2.at[1, yu * 2 + core], 5, dn_y)]
    ws += [again(pair(yd), 7, sib), again(pair(yu), 8, sib)]

    later_q.wait()
    for c in later:
        c.wait_recv()
    a_in += later
    over = send(cot.at[:, cols(1 - x, HF)], cotz.at[x, z], csem, 0, {"ctx": xb})
    u_own = send(mine_c, cotz.at[x, z], csem, 1, {"ctx": zu})
    d_own = send(mine_c, cotz.at[x, z], csem, 2, {"ctx": zd})
    y_x.append(filters(1))

    over.wait_recv()
    theirs = cotz.at[1 - x, z]
    u_oth = send(theirs, theirs, csem, 3, {"ctx": zu})
    d_oth = send(theirs, theirs, csem, 4, {"ctx": zd})

    wy[2].wait_recv()
    wy[3].wait_recv()
    ws.append(again(pair(yo), 9, sib))
    for c in ws:
        c.wait_recv()
    own_c.wait()

    def grads_of(zz):
        lhs = cotz[:, zz].reshape(2 * ROWS, HF)
        there = jnp.dot(lhs, w2[1 - x].reshape(HF, CB), preferred_element_type=F32).astype(BF16)
        here = jnp.dot(lhs, w2[x].reshape(HF, CB), preferred_element_type=F32)
        for a in range(2):
            rs = pl.ds(pl.multiple_of(a * 512 + zz * ROWS, ROWS), ROWS)
            dysend[rs, :] = there[a * ROWS : (a + 1) * ROWS]
            dypos[rs, :] = here[a * ROWS : (a + 1) * ROWS]

    d_x = []

    def send_grads(zz):
        for a in range(2):
            rs = pl.ds(pl.multiple_of(a * 512 + zz * ROWS, ROWS), ROWS)
            d_x.append(send(dysend.at[rs], dyrecv.at[rs], (d_s, d_r), len(d_x), {"ctx": xb}))

    def grads_step(n, carry):
        grads_of(lax.rem(z + 1 + 2 * n, 4))
        return carry

    grads_of(z)
    u_own.wait_recv()
    d_own.wait_recv()
    u_oth.wait_recv()
    d_oth.wait_recv()
    on_u = send(cotz.at[0, zdl], cotz.at[0, zdl], csem, 5, {"ctx": zu})
    on_d = send(cotz.at[1, zul], cotz.at[1, zul], csem, 6, {"ctx": zd})
    send_grads(z)
    lax.fori_loop(0, 2, grads_step, 0)
    send_grads(zul)
    send_grads(zdl)
    on_u.wait_recv()
    on_d.wait_recv()
    grads_of(zo)
    send_grads(zo)

    for c in y_x:
        c.wait_recv()

    def part(n, carry):
        def rows_of(b):
            return w2[b, pl.ds(n * 2, 2)].reshape(512, CB)

        val = lax.dot_general(y[:, pl.ds(0, CB)], rows_of(0), NT, preferred_element_type=F32) + lax.dot_general(
            y[:, pl.ds(CB, CB)], rows_of(1), NT, preferred_element_type=F32
        )
        for a in range(2):
            for zz in range(4):
                r0 = (a * 4 + zz) * ROWS
                parts[lax.rem(zz - z + 4, 4), a, :, cols(n, 512)] = val[r0 : r0 + ROWS].astype(BF16)
        return carry

    lax.fori_loop(0, HF // 512, part, 0)
    rsem = (r_s, r_r)
    s_u = send(parts.at[2, 0], got1.at[0], rsem, 0, {"ctx": zu})
    s_d = send(parts.at[2, 1], got1.at[1], rsem, 1, {"ctx": zd})

    vsem = (v_s, v_r)

    def weights(which, dst):
        def step(k, carry):
            lhs = cotz[:, :, :, cols(k * 2 + which, 256)].reshape(L, 256)
            val = lax.dot_general(lhs, y[...], TN, preferred_element_type=F32).astype(BF16)
            dst[k, 0] = val[:, :CB]
            dst[k, 1] = val[:, CB:]
            return carry

        lax.fori_loop(0, 4, step, 0)

    weights(1 - core, gsib)
    g_sib = send(gsib, ggot, vsem, 0, {"dp": sib})
    t_u = send(parts.at[1, 1], got2.at[0, 1], rsem, 2, {"ctx": zu})
    t_d = send(parts.at[3, 0], got2.at[1, 0], rsem, 3, {"ctx": zd})
    weights(core, gown)

    def combine(a, k):
        def fn(rs):
            fwd[a, rs, :] = (parts[k, a, rs, :].astype(F32) + got1[a, rs, :].astype(F32)).astype(BF16)

        strips(ROWS, 16, fn)

    s_u.wait_recv()
    combine(0, 1)
    f_u = send(fwd.at[0], got2.at[0, 0], rsem, 4, {"ctx": zu})
    s_d.wait_recv()
    combine(1, 3)
    f_d = send(fwd.at[1], got2.at[1, 1], rsem, 5, {"ctx": zd})

    g_sib.wait_recv()

    def add_pairs(n, carry):
        k, b = n // 2, lax.rem(n, 2)

        def fn(rs):
            gown[k, b, rs, :] = (gown[k, b, rs, :].astype(F32) + ggot[k, b, rs, :].astype(F32)).astype(BF16)

        strips(256, 64, fn)
        return carry

    lax.fori_loop(0, 8, add_pairs, 0)
    gy = [
        send(gown.at[yo, 0], ggot1.at[0], vsem, 1, {"dp": up_y}),
        send(gown.at[yo, 1], ggot1.at[1], vsem, 2, {"dp": dn_y}),
        send(gown.at[yu, 1], ggot2.at[0, 1], vsem, 3, {"dp": up_y}),
        send(gown.at[yd, 0], ggot2.at[1, 0], vsem, 4, {"dp": dn_y}),
    ]

    for c in d_x:
        c.wait_recv()

    def add_dy(rs):
        ypos[rs, :] = (dypos[rs, :] + dyrecv[rs, :].astype(F32)).astype(BF16)

    strips(L, 64, add_dy)
    dypos[pl.ds(0, L), :] = jnp.dot(perm[...], ypos[...], preferred_element_type=F32)

    def out_copy(c, n):
        p = j if n is None else peer(x, z, *A2A[n])
        src = arrived.at[:, pl.ds(pl.multiple_of(p * ROWS, ROWS), ROWS), cols(c, 128)]
        dst = dugot.at[:, :, pl.ds(pl.multiple_of(j * CB + c * 128, 128), 128)]
        if n is None:
            return pltpu.make_async_copy(src, dst, l_s.at[4 + c])
        return remote(src, dst, (q_s, q_r), c * 7 + n, {"ctx": p})

    def chunk(c, carry):
        cs = cols(c, 128)

        def backward(n, carry):
            r0 = pl.multiple_of(n * STRIP, STRIP)
            m = mask[pl.ds(r0 + PAD, STRIP + 8), :]
            q, k, v, w = [feats[a, pl.ds(r0, STRIP + PAD), cs].astype(F32)[: STRIP + 8] for a in range(4)]
            dy = dypos[pl.ds(r0, STRIP + 8), cs]

            def total(val):
                return jnp.sum(val.reshape(STRIP // 8, 8, 128), axis=0)

            b = dy * q
            zs = (k * v)[:STRIP]
            dz = inner[pl.ds(0, 1), cs] * b
            gacc[9, :, cs] += total(b[:STRIP] * zs)
            for t in range(1, 7):
                b = up(b, m)
                dz = dz + inner[pl.ds(t, 1), cs] * b
                gacc[9 + t, :, cs] += total(b[:STRIP] * zs)
            df = (dy * w, dz * v, dz * k)
            for a in range(3):
                u = upos[pl.ds(PAD + r0, STRIP), pl.ds(pl.multiple_of(a * CB + c * 128, 128), 128)].astype(F32)
                b = df[a]
                du = short[0, pl.ds(a, 1), cs] * b
                gacc[a, :, cs] += total(b[:STRIP] * u)
                for t in range(1, 3):
                    b = up(b, m)
                    du = du + short[t, pl.ds(a, 1), cs] * b
                    gacc[t * 3 + a, :, cs] += total(b[:STRIP] * u)
                dupos[pl.ds(r0, STRIP), pl.ds(a * 128, 128)] = du[:STRIP].astype(BF16)
            return carry

        lax.fori_loop(0, L // STRIP, backward, 0)
        val = lax.dot_general(perm[...], dupos[...], TN, preferred_element_type=F32).astype(BF16)
        for a in range(3):
            arrived[a, :, cs] = val[:, a * 128 : (a + 1) * 128]
        for n in range(7):
            out_copy(c, n).start()
        out_copy(c, None).start()
        return carry

    lax.fori_loop(0, 2, chunk, 0)
    gy[0].wait_recv()
    gy[1].wait_recv()
    for a, k in ((0, yu), (1, yd)):

        def add_fwd(rs):
            gfwd[a, rs, :] = (gown[k, a, rs, :].astype(F32) + ggot1[a, rs, :].astype(F32)).astype(BF16)

        strips(256, 64, add_fwd)
    gy.append(send(gfwd.at[0], ggot2.at[0, 0], vsem, 5, {"dp": up_y}))
    gy.append(send(gfwd.at[1], ggot2.at[1, 1], vsem, 6, {"dp": dn_y}))
    lax.fori_loop(2, 4, chunk, 0)

    for k in range(16):
        gall[0, pl.ds(k, 1), :] = jnp.sum(gacc[k], axis=0, keepdims=True)
    near_y = dp_id(h, yy + 1 - 2 * lax.rem(yy, 2), core)
    gx = []

    def exchange(n):
        gx.append(send(gall.at[2 * n], gall.at[2 * n + 1], (g_s, g_r), n, {"dp": (sib, near_y, over_y, flip)[n]}))

    def summed(n):
        gx[n].wait_recv()
        gall[2 * n + 2] = gall[2 * n] + gall[2 * n + 1]

    exchange(0)

    for cp in (t_u, t_d, f_u, f_d):
        cp.wait_recv()

    def finish(a, dst):
        def fn(rs):
            final[dst, rs, :] = (
                parts[0, a, rs, :].astype(F32) + (got2[0, a, rs, :].astype(F32) + got2[1, a, rs, :].astype(F32))
            ).astype(BF16)

        strips(ROWS, 16, fn)

    finish(1 - x, 0)
    m_x = send(final.at[0], mixed.at[:, cols(x, HF)], rsem, 6, {"ctx": xb})
    summed(0)
    exchange(1)
    finish(x, 1)
    m_own = pltpu.make_async_copy(final.at[1], mixed.at[:, cols(x, HF)], l_s.at[2])
    m_own.start()

    for k in range(2, 6):
        gy[k].wait_recv()
    for a in range(2):

        def add_all(rs):
            gred[a, rs, :] = (
                gown[yy, a, rs, :].astype(F32) + (ggot2[0, a, rs, :].astype(F32) + ggot2[1, a, rs, :].astype(F32))
            ).astype(BF16)

        strips(256, 64, add_all)

    def owner_copy(a):
        return remote(gred.at[a], gfin.at[h], vsem, 7 + a, {"dp": dp_id(x, yy, core), "ctx": a * 4 + z}, 7 + h)

    for a in range(2):

        @pl.when((h != x) | (x != a))
        def _():
            owner_copy(a).start()

    @pl.when(h == x)
    def _():
        def keep(rs):
            gfin[h, rs, :] = gred[x, rs, :]

        strips(256, 64, keep)

    summed(1)
    exchange(2)
    summed(2)
    exchange(3)
    summed(3)
    sums = gall[8]
    for t in range(3):
        short_out[t] = sums[t * 3 : t * 3 + 3]
    inner_out[...] = lax.dot_general(
        sums[9:16], spread, NT, preferred_element_type=F32, precision=lax.Precision.HIGHEST
    )

    for s in range(2):

        @pl.when((h != x) | (h != s))
        def _():
            remote(gred.at[0], gfin.at[s], vsem, 7, {"ctx": xb}, 7 + s).wait_recv()

    def last(rs):
        gw_out[rs, :] = gfin[0, rs, :].astype(F32) + gfin[1, rs, :].astype(F32)

    strips(256, 64, last)

    for a in range(2):

        @pl.when((h != x) | (x != a))
        def _():
            owner_copy(a).wait_send()

    @pl.when(h != x)
    def _():
        w_b.wait_send()

    m_own.wait()
    m_x.wait()
    for cp in (w_a, *wy, *ws, *a_in, over, u_own, d_own, u_oth, d_oth, on_u, on_d, *y_x, *d_x):
        cp.wait_send()
    for cp in (s_u, s_d, t_u, t_d, f_u, f_d, g_sib, *gy, *gx):
        cp.wait_send()
    for c in range(4):
        for n in (*range(7), None):
            out_copy(c, n).wait()


VM = pl.BlockSpec(memory_space=pltpu.VMEM)
SM = pl.BlockSpec(memory_space=pltpu.SMEM)
HB = pl.BlockSpec(memory_space=pl.ANY)
DMA = pltpu.SemaphoreType.DMA
NT = (((1,), (1,)), ((), ()))
TN = (((0,), (0,)), ((), ()))


def sems(*counts):
    return [DMA((n,)) for n in counts for _ in range(2)]


def block(qs, cot, wt, order_row, lens, short, inner):
    sds = jax.ShapeDtypeStruct
    vm = pltpu.VMEM
    return pl.pallas_call(
        block_kernel,
        out_shape=(
            sds((ROWS, 2 * HF), BF16),
            sds((3, ROWS, 8 * CB), BF16),
            sds((256, CB), F32),
            sds((3, 3, CB), F32),
            sds((7, CB // GROUP), F32),
        ),
        in_specs=[HB, HB, HB, VM, SM, VM, VM],
        out_specs=(HB, HB, VM, VM, VM),
        scratch_shapes=[
            vm((3, L, CB), BF16),
            vm((L + 2 * PAD, 3 * CB), BF16),
            vm((4, L + PAD, CB), BF16),
            vm((L, L), BF16),
            vm((L + 2 * PAD, 128), F32),
            vm((L, CB), BF16),
            vm((L, 2 * CB), BF16),
            vm((2, 4, ROWS, HF), BF16),
            vm((2, 8, 256, CB), BF16),
            vm((7, CB), F32),
            vm((L, CB), BF16),
            vm((L, CB), BF16),
            vm((L + 8, CB), F32),
            vm((L, 384), BF16),
            vm((4, 2, ROWS, HF), BF16),
            vm((2, ROWS, HF), BF16),
            vm((2, ROWS, HF), BF16),
            vm((2, 2, ROWS, HF), BF16),
            vm((2, ROWS, HF), BF16),
            vm((16, 8, CB), F32),
            vm((9, 16, CB), F32),
            vm((4, 2, 256, CB), BF16),
            vm((4, 2, 256, CB), BF16),
            vm((4, 2, 256, CB), BF16),
            vm((2, 256, CB), BF16),
            vm((2, 256, CB), BF16),
            vm((2, 2, 256, CB), BF16),
            vm((2, 256, CB), BF16),
            vm((2, 256, CB), BF16),
            *sems(14, 9, 10, 7, 28, 4, 9, 8),
            DMA((9,)),
        ],
        compiler_params=pltpu.CompilerParams(collective_id=0, has_side_effects=True, vmem_limit_bytes=60 << 20),
        cost_estimate=pl.CostEstimate(flops=30 << 30, bytes_accessed=100 << 20, transcendentals=0),
        name="block",
    )(qs, cot, wt, order_row, lens, short, inner)


def on_device(qkv, short_filter, inner_filter, out_weight, cotangent, order, lengths):
    qs = qkv.transpose(1, 0, 2)
    mixed, dugot, gw, grad_short, grad_inner = block(
        qs, cotangent, out_weight, order, lengths, short_filter, inner_filter
    )
    return (mixed, dugot.transpose(1, 0, 2), gw, grad_short, grad_inner)


def solution(mesh):
    in_specs = (
        P(("dp", "ctx"), None, None),
        P(None, None, "ctx"),
        P(None, "ctx"),
        P("dp", "ctx"),
        P(("dp", "ctx"), None),
        P("dp", None),
        P("dp", None),
    )
    out_specs = (
        P(("dp", "ctx"), None),
        P(("dp", "ctx"), None, None),
        P("dp", "ctx"),
        P(None, None, "ctx"),
        P(None, "ctx"),
    )
    return jax.shard_map(on_device, mesh=mesh, in_specs=in_specs, out_specs=out_specs, check_vma=False)
```

```python
import jax
import jax.numpy as jnp
from jax import lax
from jax.sharding import PartitionSpec as P
from jax.experimental import pallas as pl
from jax.experimental.pallas import tpu as pltpu

MESH = pl.DeviceIdType.MESH
F32 = jnp.float32
BF16 = jnp.bfloat16
GROUP = 16
L = 1024
CB = 512
HF = 2048
ROWS = 128
PAD = 16
STRIP = 128
A2A = ((0, 2), (1, 2), (1, 1), (1, 3), (0, 1), (0, 3), (1, 0))


def where_am_i():
    j = lax.axis_index("ctx")
    return j, j // 4, lax.rem(j, 4)


def peer(x, z, dx, dz):
    return lax.rem(x + dx, 2) * 4 + lax.rem(z + dz, 4)


def barrier(ids):
    sem = pltpu.get_barrier_semaphore()
    for d in ids:
        pl.semaphore_signal(sem, inc=1, device_id=d, device_id_type=MESH)
    pl.semaphore_wait(sem, len(ids))


def fill_masks(lens_ref, m_ref):
    p = lax.broadcasted_iota(jnp.int32, m_ref.shape, 0) - PAD
    good = (p > 0) & (p < L)
    end = jnp.int32(0)
    for k in range(lens_ref.shape[1]):
        end = end + lens_ref[0, k]
        good = good & (p != end)
    m_ref[...] = jnp.where(good, 1.0, 0.0).astype(F32)


def fill_gather(order_row_ref, out_ref):
    def step(i, c):
        r0 = pl.multiple_of(i * 128, 128)
        p = lax.broadcasted_iota(jnp.int32, (128, L), 0) + r0
        out_ref[pl.ds(r0, 128), :] = jnp.where(p == order_row_ref[...], 1.0, 0.0).astype(BF16)
        return c

    lax.fori_loop(0, L // 128, step, 0)


def down(x, m):
    return pltpu.roll(x, 1, 0) * m


def up(x, m):
    return pltpu.roll(x * m, x.shape[0] - 1, 0)


def taps3(u, m, filt):
    u1 = down(u, m)
    u2 = down(u1, m)
    return filt[0] * u + filt[1] * u1 + filt[2] * u2


def dp_id(h, yy, c):
    return h * 8 + yy * 2 + c


def coords():
    i = lax.axis_index("dp")
    return i, i // 8, lax.rem(i // 2, 4), lax.rem(i, 2)


def strips(rows, step, fn):
    def body(n, carry):
        fn(pl.ds(pl.multiple_of(n * step, step), step))
        return carry

    lax.fori_loop(0, rows // step, body, 0)


def block_kernel(
    qs, cot, wt, order_row, lens, short, inner_g,
    mixed, dugot, gw_out, short_out, inner_out,
    arrived, upos, feats, perm, mask, ypos, y, cotz, w2, inner,
    dysend, dyrecv, dypos, dupos,
    parts, fwd, got1, got2, final, gacc, gall,
    gsib, ggot, gown, gfwd, ggot1, ggot2, gred, gfin,
    a_s, a_r, c_s, c_r, w_s, w_r, r_s, r_r, q_s, q_r, g_s, g_r, v_s, v_r, d_s, d_r, l_s,
):
    j, x, z = where_am_i()
    i, h, yy, core = coords()
    xb = peer(x, z, 1, 0)
    zul, zdl, zo = lax.rem(z + 1, 4), lax.rem(z + 3, 4), lax.rem(z + 2, 4)
    zu, zd = x * 4 + zul, x * 4 + zdl
    yu, yd, yo = lax.rem(yy + 1, 4), lax.rem(yy + 3, 4), lax.rem(yy + 2, 4)
    up_y, dn_y, sib = dp_id(h, yu, core), dp_id(h, yd, core), dp_id(h, yy, 1 - core)
    over_y, flip = dp_id(h, yo, core), dp_id(1 - h, yy, core)
    barrier(
        [{"ctx": peer(x, z, dx, dz)} for dx, dz in A2A]
        + [{"dp": up_y}, {"dp": dn_y}, {"dp": over_y}, {"dp": sib}, {"dp": flip}]
        + [{"dp": flip, "ctx": xb}]
    )

    def remote(src, dst, sems, n, to, rn=None):
        return pltpu.make_async_remote_copy(
            src, dst, sems[0].at[n], sems[1].at[n if rn is None else rn], device_id=to, device_id_type=MESH
        )

    def send(src, dst, sems, n, to, rn=None):
        c = remote(src, dst, sems, n, to, rn)
        c.start()
        return c

    def cols(k, width):
        return pl.ds(pl.multiple_of(k * width, width), width)

    wsem = (w_s, w_r)
    w_mine = w2.at[x, yy * 2 + core]
    w_a = send(wt, w_mine, wsem, 0, {"dp": flip, "ctx": h * 4 + z}, x)
    w_b = remote(wt, w_mine, wsem, 1, {"ctx": h * 4 + z}, x)
    w_l = pltpu.make_async_copy(wt, w_mine, l_s.at[3])

    @pl.when(h != x)
    def _():
        w_b.start()

    @pl.when(h == x)
    def _():
        w_l.start()

    mine_rows = pl.ds(pl.multiple_of(j * ROWS, ROWS), ROWS)

    def streams_in(half):
        made = []
        here = arrived.at[:, mine_rows, pl.ds(half * 256, 256)]

        def block_of(p):
            return qs.at[:, :, pl.ds(pl.multiple_of(p * CB + half * 256, 256), 256)]

        for n, (dx, dz) in enumerate(A2A):
            p = peer(x, z, dx, dz)
            made.append(send(block_of(p), here, (a_s, a_r), half * 7 + n, {"ctx": p}))
        own = pltpu.make_async_copy(block_of(j), here, l_s.at[(0, 8)[half]])
        own.start()
        return made, own

    a_in, own_q = streams_in(0)
    mine_c = cot.at[:, cols(x, HF)]
    own_c = pltpu.make_async_copy(mine_c, cotz.at[x, z], l_s.at[1])
    own_c.start()

    fill_masks(lens, mask)
    fill_gather(order_row, perm)
    upos[pl.ds(0, PAD), :] = jnp.zeros((PAD, 3 * CB), BF16)
    upos[pl.ds(PAD + L, PAD), :] = jnp.zeros((PAD, 3 * CB), BF16)
    feats[:, pl.ds(L, PAD), :] = jnp.zeros((4, PAD, CB), BF16)
    gacc[...] = jnp.zeros_like(gacc)
    dypos[pl.ds(L, 8), :] = jnp.zeros((8, CB), F32)
    group_of = lax.broadcasted_iota(jnp.int32, (CB // GROUP, CB), 1) // GROUP
    spread = jnp.where(group_of == lax.broadcasted_iota(jnp.int32, (CB // GROUP, CB), 0), 1.0, 0.0).astype(F32)
    inner[...] = jnp.dot(inner_g[...], spread, preferred_element_type=F32, precision=lax.Precision.HIGHEST)

    remote(wt, w2.at[1 - x, yy * 2 + core], wsem, 0, {"ctx": xb}, 1 - x).wait_recv()

    @pl.when(h != x)
    def _():
        remote(wt, w_mine, wsem, 0, {"ctx": xb}, x).wait_recv()

    @pl.when(h == x)
    def _():
        w_l.wait()

    def pair(k):
        return w2.at[:, k * 2 + core]

    def again(ref, n, to):
        return send(ref, ref, wsem, n, {"dp": to})

    wy = [again(pair(yy), 2, up_y), again(pair(yy), 3, dn_y)]
    ws = [again(pair(yy), 6, sib)]
    later, later_q = streams_in(1)

    def filters(half):
        def place(a, c):
            upos[pl.ds(PAD, L), pl.ds(pl.multiple_of(a * CB + half * 256, 256), 256)] = jnp.dot(
                perm[...], arrived[a, :, pl.ds(half * 256, 256)], preferred_element_type=F32
            ).astype(BF16)
            return c

        lax.fori_loop(0, 3, place, 0)

        def forward(n, carry):
            c0 = pl.multiple_of(half * 256 + lax.rem(n, 2) * 128, 128)
            cs = pl.ds(c0, 128)
            r0 = pl.multiple_of((n // 2) * STRIP, STRIP)
            m = mask[pl.ds(r0 + 8, STRIP + 8), :]
            made = []
            for a in range(3):
                u = upos[pl.ds(r0, STRIP + PAD), pl.ds(a * CB + c0, 128)].astype(F32)[8:]
                made.append(taps3(u, m, [short[t, pl.ds(a, 1), cs] for t in range(3)]))
            q, k, v = made
            zt = k * v
            w = inner[pl.ds(0, 1), cs] * zt
            for t in range(1, 7):
                zt = down(zt, m)
                w = w + inner[pl.ds(t, 1), cs] * zt
            for a, val in enumerate((q, k, v, w)):
                feats[a, pl.ds(r0, STRIP), cs] = val[8:].astype(BF16)
            ypos[pl.ds(r0, STRIP), cs] = (q * w)[8:].astype(BF16)
            return carry

        lax.fori_loop(0, 2 * (L // STRIP), forward, 0)
        my_y = pl.ds(pl.multiple_of(x * CB + half * 256, 256), 256)
        y[:, my_y] = lax.dot_general(
            perm[...], ypos[:, pl.ds(half * 256, 256)], TN, preferred_element_type=F32
        ).astype(BF16)
        return send(y.at[:, my_y], y.at[:, my_y], csem, 7 + half, {"ctx": xb})

    csem = (c_s, c_r)
    own_q.wait()
    for c in a_in:
        c.wait_recv()
    y_x = [filters(0)]

    wy[0].wait_recv()
    wy[1].wait_recv()
    wy += [again(w2.at[0, yd * 2 + core], 4, up_y), again(w2.at[1, yu * 2 + core], 5, dn_y)]
    ws += [again(pair(yd), 7, sib), again(pair(yu), 8, sib)]

    later_q.wait()
    for c in later:
        c.wait_recv()
    a_in += later
    over = send(cot.at[:, cols(1 - x, HF)], cotz.at[x, z], csem, 0, {"ctx": xb})
    u_own = send(mine_c, cotz.at[x, z], csem, 1, {"ctx": zu})
    d_own = send(mine_c, cotz.at[x, z], csem, 2, {"ctx": zd})
    y_x.append(filters(1))

    over.wait_recv()
    theirs = cotz.at[1 - x, z]
    u_oth = send(theirs, theirs, csem, 3, {"ctx": zu})
    d_oth = send(theirs, theirs, csem, 4, {"ctx": zd})

    wy[2].wait_recv()
    wy[3].wait_recv()
    ws.append(again(pair(yo), 9, sib))
    for c in ws:
        c.wait_recv()
    own_c.wait()

    def grads_of(zz):
        lhs = cotz[:, zz].reshape(2 * ROWS, HF)
        there = jnp.dot(lhs, w2[1 - x].reshape(HF, CB), preferred_element_type=F32).astype(BF16)
        here = jnp.dot(lhs, w2[x].reshape(HF, CB), preferred_element_type=F32)
        for a in range(2):
            rs = pl.ds(pl.multiple_of(a * 512 + zz * ROWS, ROWS), ROWS)
            dysend[rs, :] = there[a * ROWS : (a + 1) * ROWS]
            dypos[rs, :] = here[a * ROWS : (a + 1) * ROWS]

    d_x = []

    def send_grads(zz):
        for a in range(2):
            rs = pl.ds(pl.multiple_of(a * 512 + zz * ROWS, ROWS), ROWS)
            d_x.append(send(dysend.at[rs], dyrecv.at[rs], (d_s, d_r), len(d_x), {"ctx": xb}))

    def grads_step(n, carry):
        grads_of(lax.rem(z + 1 + 2 * n, 4))
        return carry

    grads_of(z)
    u_own.wait_recv()
    d_own.wait_recv()
    u_oth.wait_recv()
    d_oth.wait_recv()
    on_u = send(cotz.at[0, zdl], cotz.at[0, zdl], csem, 5, {"ctx": zu})
    on_d = send(cotz.at[1, zul], cotz.at[1, zul], csem, 6, {"ctx": zd})
    lax.fori_loop(0, 2, grads_step, 0)

    def outputs(blocks, again_):
        def part(n, carry):
            val = None
            for b, c0, width in blocks:
                term = lax.dot_general(
                    y[:, pl.ds(pl.multiple_of(b * CB + c0, 256), width)],
                    w2[b, pl.ds(n * 2, 2), :, pl.ds(c0, width)].reshape(512, width),
                    NT,
                    preferred_element_type=F32,
                )
                val = term if val is None else val + term
            for a in range(2):
                for zz in range(4):
                    r0 = (a * 4 + zz) * ROWS
                    place = (lax.rem(zz - z + 4, 4), a, slice(None), cols(n, 512))
                    rows = val[r0 : r0 + ROWS]
                    parts[place] = (rows + parts[place].astype(F32) if again_ else rows).astype(BF16)
            return carry

        lax.fori_loop(0, HF // 512, part, 0)

    y_x[0].wait_recv()
    outputs(((x, 0, CB), (1 - x, 0, 256)), False)
    on_u.wait_recv()
    on_d.wait_recv()
    grads_of(zo)

    y_x[1].wait_recv()
    for k in (zo, z, zul, zdl):
        send_grads(k)
    outputs(((1 - x, 256, 256),), True)

    rsem = (r_s, r_r)
    s_u = send(parts.at[2, 0], got1.at[0], rsem, 0, {"ctx": zu})
    s_d = send(parts.at[2, 1], got1.at[1], rsem, 1, {"ctx": zd})

    vsem = (v_s, v_r)

    def weights(which, dst):
        def step(k, carry):
            lhs = cotz[:, :, :, cols(k * 2 + which, 256)].reshape(L, 256)
            val = lax.dot_general(lhs, y[...], TN, preferred_element_type=F32).astype(BF16)
            dst[k, 0] = val[:, :CB]
            dst[k, 1] = val[:, CB:]
            return carry

        lax.fori_loop(0, 4, step, 0)

    weights(1 - core, gsib)
    g_sib = send(gsib, ggot, vsem, 0, {"dp": sib})
    t_u = send(parts.at[1, 1], got2.at[0, 1], rsem, 2, {"ctx": zu})
    t_d = send(parts.at[3, 0], got2.at[1, 0], rsem, 3, {"ctx": zd})
    weights(core, gown)

    def combine(a, k):
        def fn(rs):
            fwd[a, rs, :] = (parts[k, a, rs, :].astype(F32) + got1[a, rs, :].astype(F32)).astype(BF16)

        strips(ROWS, 16, fn)

    s_u.wait_recv()
    combine(0, 1)
    f_u = send(fwd.at[0], got2.at[0, 0], rsem, 4, {"ctx": zu})
    s_d.wait_recv()
    combine(1, 3)
    f_d = send(fwd.at[1], got2.at[1, 1], rsem, 5, {"ctx": zd})

    g_sib.wait_recv()

    def add_pairs(n, carry):
        k, b = n // 2, lax.rem(n, 2)

        def fn(rs):
            gown[k, b, rs, :] = (gown[k, b, rs, :].astype(F32) + ggot[k, b, rs, :].astype(F32)).astype(BF16)

        strips(256, 64, fn)
        return carry

    lax.fori_loop(0, 8, add_pairs, 0)
    gy = [
        send(gown.at[yo, 0], ggot1.at[0], vsem, 1, {"dp": up_y}),
        send(gown.at[yo, 1], ggot1.at[1], vsem, 2, {"dp": dn_y}),
        send(gown.at[yu, 1], ggot2.at[0, 1], vsem, 3, {"dp": up_y}),
        send(gown.at[yd, 0], ggot2.at[1, 0], vsem, 4, {"dp": dn_y}),
    ]

    for c in d_x:
        c.wait_recv()

    def add_dy(rs):
        ypos[rs, :] = (dypos[rs, :] + dyrecv[rs, :].astype(F32)).astype(BF16)

    strips(L, 64, add_dy)
    dypos[pl.ds(0, L), :] = jnp.dot(perm[...], ypos[...], preferred_element_type=F32)

    def out_copy(c, n):
        p = j if n is None else peer(x, z, *A2A[n])
        src = arrived.at[:, pl.ds(pl.multiple_of(p * ROWS, ROWS), ROWS), cols(c, 128)]
        dst = dugot.at[:, :, pl.ds(pl.multiple_of(j * CB + c * 128, 128), 128)]
        if n is None:
            return pltpu.make_async_copy(src, dst, l_s.at[4 + c])
        return remote(src, dst, (q_s, q_r), c * 7 + n, {"ctx": p})

    def chunk(c, carry):
        cs = cols(c, 128)

        def backward(n, carry):
            r0 = pl.multiple_of(n * STRIP, STRIP)
            m = mask[pl.ds(r0 + PAD, STRIP + 8), :]
            q, k, v, w = [feats[a, pl.ds(r0, STRIP + PAD), cs].astype(F32)[: STRIP + 8] for a in range(4)]
            dy = dypos[pl.ds(r0, STRIP + 8), cs]

            def total(val):
                return jnp.sum(val.reshape(STRIP // 8, 8, 128), axis=0)

            b = dy * q
            zs = (k * v)[:STRIP]
            dz = inner[pl.ds(0, 1), cs] * b
            gacc[9, :, cs] += total(b[:STRIP] * zs)
            for t in range(1, 7):
                b = up(b, m)
                dz = dz + inner[pl.ds(t, 1), cs] * b
                gacc[9 + t, :, cs] += total(b[:STRIP] * zs)
            df = (dy * w, dz * v, dz * k)
            for a in range(3):
                u = upos[pl.ds(PAD + r0, STRIP), pl.ds(pl.multiple_of(a * CB + c * 128, 128), 128)].astype(F32)
                b = df[a]
                du = short[0, pl.ds(a, 1), cs] * b
                gacc[a, :, cs] += total(b[:STRIP] * u)
                for t in range(1, 3):
                    b = up(b, m)
                    du = du + short[t, pl.ds(a, 1), cs] * b
                    gacc[t * 3 + a, :, cs] += total(b[:STRIP] * u)
                dupos[pl.ds(r0, STRIP), pl.ds(a * 128, 128)] = du[:STRIP].astype(BF16)
            return carry

        lax.fori_loop(0, L // STRIP, backward, 0)
        val = lax.dot_general(perm[...], dupos[...], TN, preferred_element_type=F32).astype(BF16)
        for a in range(3):
            arrived[a, :, cs] = val[:, a * 128 : (a + 1) * 128]
        for n in range(7):
            out_copy(c, n).start()
        out_copy(c, None).start()
        return carry

    lax.fori_loop(0, 2, chunk, 0)
    gy[0].wait_recv()
    gy[1].wait_recv()
    for a, k in ((0, yu), (1, yd)):

        def add_fwd(rs):
            gfwd[a, rs, :] = (gown[k, a, rs, :].astype(F32) + ggot1[a, rs, :].astype(F32)).astype(BF16)

        strips(256, 64, add_fwd)
    gy.append(send(gfwd.at[0], ggot2.at[0, 0], vsem, 5, {"dp": up_y}))
    gy.append(send(gfwd.at[1], ggot2.at[1, 1], vsem, 6, {"dp": dn_y}))
    lax.fori_loop(2, 4, chunk, 0)

    for k in range(16):
        gall[0, pl.ds(k, 1), :] = jnp.sum(gacc[k], axis=0, keepdims=True)
    near_y = dp_id(h, yy + 1 - 2 * lax.rem(yy, 2), core)
    gx = []

    def exchange(n):
        gx.append(send(gall.at[2 * n], gall.at[2 * n + 1], (g_s, g_r), n, {"dp": (sib, near_y, over_y, flip)[n]}))

    def summed(n):
        gx[n].wait_recv()
        gall[2 * n + 2] = gall[2 * n] + gall[2 * n + 1]

    exchange(0)

    for cp in (t_u, t_d, f_u, f_d):
        cp.wait_recv()

    def finish(a, dst):
        def fn(rs):
            final[dst, rs, :] = (
                parts[0, a, rs, :].astype(F32) + (got2[0, a, rs, :].astype(F32) + got2[1, a, rs, :].astype(F32))
            ).astype(BF16)

        strips(ROWS, 16, fn)

    finish(1 - x, 0)
    m_x = send(final.at[0], mixed.at[:, cols(x, HF)], rsem, 6, {"ctx": xb})
    summed(0)
    exchange(1)
    finish(x, 1)
    m_own = pltpu.make_async_copy(final.at[1], mixed.at[:, cols(x, HF)], l_s.at[2])
    m_own.start()

    for k in range(2, 6):
        gy[k].wait_recv()
    for a in range(2):

        def add_all(rs):
            gred[a, rs, :] = (
                gown[yy, a, rs, :].astype(F32) + (ggot2[0, a, rs, :].astype(F32) + ggot2[1, a, rs, :].astype(F32))
            ).astype(BF16)

        strips(256, 64, add_all)

    def owner_copy(a):
        return remote(gred.at[a], gfin.at[h], vsem, 7 + a, {"dp": dp_id(x, yy, core), "ctx": a * 4 + z}, 7 + h)

    for a in range(2):

        @pl.when((h != x) | (x != a))
        def _():
            owner_copy(a).start()

    @pl.when(h == x)
    def _():
        def keep(rs):
            gfin[h, rs, :] = gred[x, rs, :]

        strips(256, 64, keep)

    summed(1)
    exchange(2)
    summed(2)
    exchange(3)
    summed(3)
    sums = gall[8]
    for t in range(3):
        short_out[t] = sums[t * 3 : t * 3 + 3]
    inner_out[...] = lax.dot_general(
        sums[9:16], spread, NT, preferred_element_type=F32, precision=lax.Precision.HIGHEST
    )

    for s in range(2):

        @pl.when((h != x) | (h != s))
        def _():
            remote(gred.at[0], gfin.at[s], vsem, 7, {"ctx": xb}, 7 + s).wait_recv()

    def last(rs):
        gw_out[rs, :] = gfin[0, rs, :].astype(F32) + gfin[1, rs, :].astype(F32)

    strips(256, 64, last)

    for a in range(2):

        @pl.when((h != x) | (x != a))
        def _():
            owner_copy(a).wait_send()

    @pl.when(h != x)
    def _():
        w_b.wait_send()

    m_own.wait()
    m_x.wait()
    for cp in (w_a, *wy, *ws, *a_in, over, u_own, d_own, u_oth, d_oth, on_u, on_d, *y_x, *d_x):
        cp.wait_send()
    for cp in (s_u, s_d, t_u, t_d, f_u, f_d, g_sib, *gy, *gx):
        cp.wait_send()
    for c in range(4):
        for n in (*range(7), None):
            out_copy(c, n).wait()


VM = pl.BlockSpec(memory_space=pltpu.VMEM)
SM = pl.BlockSpec(memory_space=pltpu.SMEM)
HB = pl.BlockSpec(memory_space=pl.ANY)
DMA = pltpu.SemaphoreType.DMA
NT = (((1,), (1,)), ((), ()))
TN = (((0,), (0,)), ((), ()))


def sems(*counts):
    return [DMA((n,)) for n in counts for _ in range(2)]


def block(qs, cot, wt, order_row, lens, short, inner):
    sds = jax.ShapeDtypeStruct
    vm = pltpu.VMEM
    return pl.pallas_call(
        block_kernel,
        out_shape=(
            sds((ROWS, 2 * HF), BF16),
            sds((3, ROWS, 8 * CB), BF16),
            sds((256, CB), F32),
            sds((3, 3, CB), F32),
            sds((7, CB // GROUP), F32),
        ),
        in_specs=[HB, HB, HB, VM, SM, VM, VM],
        out_specs=(HB, HB, VM, VM, VM),
        scratch_shapes=[
            vm((3, L, CB), BF16),
            vm((L + 2 * PAD, 3 * CB), BF16),
            vm((4, L + PAD, CB), BF16),
            vm((L, L), BF16),
            vm((L + 2 * PAD, 128), F32),
            vm((L, CB), BF16),
            vm((L, 2 * CB), BF16),
            vm((2, 4, ROWS, HF), BF16),
            vm((2, 8, 256, CB), BF16),
            vm((7, CB), F32),
            vm((L, CB), BF16),
            vm((L, CB), BF16),
            vm((L + 8, CB), F32),
            vm((L, 384), BF16),
            vm((4, 2, ROWS, HF), BF16),
            vm((2, ROWS, HF), BF16),
            vm((2, ROWS, HF), BF16),
            vm((2, 2, ROWS, HF), BF16),
            vm((2, ROWS, HF), BF16),
            vm((16, 8, CB), F32),
            vm((9, 16, CB), F32),
            vm((4, 2, 256, CB), BF16),
            vm((4, 2, 256, CB), BF16),
            vm((4, 2, 256, CB), BF16),
            vm((2, 256, CB), BF16),
            vm((2, 256, CB), BF16),
            vm((2, 2, 256, CB), BF16),
            vm((2, 256, CB), BF16),
            vm((2, 256, CB), BF16),
            *sems(14, 9, 10, 7, 28, 4, 9, 8),
            DMA((9,)),
        ],
        compiler_params=pltpu.CompilerParams(collective_id=0, has_side_effects=True, vmem_limit_bytes=60 << 20),
        cost_estimate=pl.CostEstimate(flops=30 << 30, bytes_accessed=100 << 20, transcendentals=0),
        name="block",
    )(qs, cot, wt, order_row, lens, short, inner)


def on_device(qkv, short_filter, inner_filter, out_weight, cotangent, order, lengths):
    qs = qkv.transpose(1, 0, 2)
    mixed, dugot, gw, grad_short, grad_inner = block(
        qs, cotangent, out_weight, order, lengths, short_filter, inner_filter
    )
    return (mixed, dugot.transpose(1, 0, 2), gw, grad_short, grad_inner)


def solution(mesh):
    in_specs = (
        P(("dp", "ctx"), None, None),
        P(None, None, "ctx"),
        P(None, "ctx"),
        P("dp", "ctx"),
        P(("dp", "ctx"), None),
        P("dp", None),
        P("dp", None),
    )
    out_specs = (
        P(("dp", "ctx"), None),
        P(("dp", "ctx"), None, None),
        P("dp", "ctx"),
        P(None, None, "ctx"),
        P(None, "ctx"),
    )
    return jax.shard_map(on_device, mesh=mesh, in_specs=in_specs, out_specs=out_specs, check_vma=False)
```

```python
import jax
import jax.numpy as jnp
from jax import lax
from jax.sharding import PartitionSpec as P
from jax.experimental import pallas as pl
from jax.experimental.pallas import tpu as pltpu

MESH = pl.DeviceIdType.MESH
F32 = jnp.float32
BF16 = jnp.bfloat16
GROUP = 16
L = 1024
CB = 512
HF = 2048
ROWS = 128
PAD = 16
STRIP = 128
A2A = ((0, 2), (1, 2), (1, 1), (1, 3), (0, 1), (0, 3), (1, 0))


def where_am_i():
    j = lax.axis_index("ctx")
    return j, j // 4, lax.rem(j, 4)


def peer(x, z, dx, dz):
    return lax.rem(x + dx, 2) * 4 + lax.rem(z + dz, 4)


def barrier(ids):
    sem = pltpu.get_barrier_semaphore()
    for d in ids:
        pl.semaphore_signal(sem, inc=1, device_id=d, device_id_type=MESH)
    pl.semaphore_wait(sem, len(ids))


def fill_masks(lens_ref, m_ref):
    p = lax.broadcasted_iota(jnp.int32, m_ref.shape, 0) - PAD
    good = (p > 0) & (p < L)
    end = jnp.int32(0)
    for k in range(lens_ref.shape[1]):
        end = end + lens_ref[0, k]
        good = good & (p != end)
    m_ref[...] = jnp.where(good, 1.0, 0.0).astype(F32)


def fill_gather(order_row_ref, out_ref):
    def step(i, c):
        r0 = pl.multiple_of(i * 128, 128)
        p = lax.broadcasted_iota(jnp.int32, (128, L), 0) + r0
        out_ref[pl.ds(r0, 128), :] = jnp.where(p == order_row_ref[...], 1.0, 0.0).astype(BF16)
        return c

    lax.fori_loop(0, L // 128, step, 0)


def down(x, m):
    return pltpu.roll(x, 1, 0) * m


def up(x, m):
    return pltpu.roll(x * m, x.shape[0] - 1, 0)


def taps3(u, m, filt):
    u1 = down(u, m)
    u2 = down(u1, m)
    return filt[0] * u + filt[1] * u1 + filt[2] * u2


def dp_id(h, yy, c):
    return h * 8 + yy * 2 + c


def coords():
    i = lax.axis_index("dp")
    return i, i // 8, lax.rem(i // 2, 4), lax.rem(i, 2)


def strips(rows, step, fn):
    def body(n, carry):
        fn(pl.ds(pl.multiple_of(n * step, step), step))
        return carry

    lax.fori_loop(0, rows // step, body, 0)


def block_kernel(
    qs, cot, wt, order_row, lens, short, inner_g,
    mixed, dugot, gw_out, short_out, inner_out,
    arrived, upos, feats, perm, mask, ypos, y, cotz, w2, inner,
    dysend, dyrecv, dypos, dupos,
    parts, fwd, got1, got2, final, gacc, gall,
    gsib, ggot, gown, gfwd, ggot1, ggot2, gred, gfin,
    a_s, a_r, c_s, c_r, w_s, w_r, r_s, r_r, q_s, q_r, g_s, g_r, v_s, v_r, d_s, d_r, l_s,
):
    j, x, z = where_am_i()
    i, h, yy, core = coords()
    xb = peer(x, z, 1, 0)
    zul, zdl, zo = lax.rem(z + 1, 4), lax.rem(z + 3, 4), lax.rem(z + 2, 4)
    zu, zd = x * 4 + zul, x * 4 + zdl
    yu, yd, yo = lax.rem(yy + 1, 4), lax.rem(yy + 3, 4), lax.rem(yy + 2, 4)
    up_y, dn_y, sib = dp_id(h, yu, core), dp_id(h, yd, core), dp_id(h, yy, 1 - core)
    over_y, flip = dp_id(h, yo, core), dp_id(1 - h, yy, core)
    barrier(
        [{"ctx": peer(x, z, dx, dz)} for dx, dz in A2A]
        + [{"dp": up_y}, {"dp": dn_y}, {"dp": over_y}, {"dp": sib}, {"dp": flip}]
        + [{"dp": flip, "ctx": xb}]
    )

    def remote(src, dst, sems, n, to, rn=None):
        return pltpu.make_async_remote_copy(
            src, dst, sems[0].at[n], sems[1].at[n if rn is None else rn], device_id=to, device_id_type=MESH
        )

    def send(src, dst, sems, n, to, rn=None):
        c = remote(src, dst, sems, n, to, rn)
        c.start()
        return c

    def cols(k, width):
        return pl.ds(pl.multiple_of(k * width, width), width)

    wsem = (w_s, w_r)
    w_mine = w2.at[x, yy * 2 + core]
    w_a = send(wt, w_mine, wsem, 0, {"dp": flip, "ctx": h * 4 + z}, x)
    w_b = remote(wt, w_mine, wsem, 1, {"ctx": h * 4 + z}, x)
    w_l = pltpu.make_async_copy(wt, w_mine, l_s.at[3])

    @pl.when(h != x)
    def _():
        w_b.start()

    @pl.when(h == x)
    def _():
        w_l.start()

    mine_rows = pl.ds(pl.multiple_of(j * ROWS, ROWS), ROWS)
    a_in = []
    for n, (dx, dz) in enumerate(A2A):
        p = peer(x, z, dx, dz)
        a_in.append(send(qs.at[:, :, cols(p, CB)], arrived.at[:, mine_rows, :], (a_s, a_r), n, {"ctx": p}))
    own_q = pltpu.make_async_copy(qs.at[:, :, cols(j, CB)], arrived.at[:, mine_rows, :], l_s.at[0])
    own_q.start()

    mine_c = cot.at[:, cols(x, HF)]
    own_c = pltpu.make_async_copy(mine_c, cotz.at[x, z], l_s.at[1])
    own_c.start()

    fill_masks(lens, mask)
    fill_gather(order_row, perm)
    upos[pl.ds(0, PAD), :] = jnp.zeros((PAD, 3 * CB), BF16)
    upos[pl.ds(PAD + L, PAD), :] = jnp.zeros((PAD, 3 * CB), BF16)
    feats[:, pl.ds(L, PAD), :] = jnp.zeros((4, PAD, CB), BF16)
    gacc[...] = jnp.zeros_like(gacc)
    dypos[pl.ds(L, 8), :] = jnp.zeros((8, CB), F32)
    group_of = lax.broadcasted_iota(jnp.int32, (CB // GROUP, CB), 1) // GROUP
    spread = jnp.where(group_of == lax.broadcasted_iota(jnp.int32, (CB // GROUP, CB), 0), 1.0, 0.0).astype(F32)
    inner[...] = jnp.dot(inner_g[...], spread, preferred_element_type=F32, precision=lax.Precision.HIGHEST)

    remote(wt, w2.at[1 - x, yy * 2 + core], wsem, 0, {"ctx": xb}, 1 - x).wait_recv()

    @pl.when(h != x)
    def _():
        remote(wt, w_mine, wsem, 0, {"ctx": xb}, x).wait_recv()

    @pl.when(h == x)
    def _():
        w_l.wait()

    def pair(k):
        return w2.at[:, k * 2 + core]

    def again(ref, n, to):
        return send(ref, ref, wsem, n, {"dp": to})

    wy = [again(pair(yy), 2, up_y), again(pair(yy), 3, dn_y)]
    ws = [again(pair(yy), 6, sib)]
    wy[0].wait_recv()
    wy[1].wait_recv()
    wy += [again(w2.at[0, yd * 2 + core], 4, up_y), again(w2.at[1, yu * 2 + core], 5, dn_y)]
    ws += [again(pair(yd), 7, sib), again(pair(yu), 8, sib)]

    own_q.wait()
    for c in a_in:
        c.wait_recv()

    csem = (c_s, c_r)
    over = send(cot.at[:, cols(1 - x, HF)], cotz.at[x, z], csem, 0, {"ctx": xb})
    u_own = send(mine_c, cotz.at[x, z], csem, 1, {"ctx": zu})
    d_own = send(mine_c, cotz.at[x, z], csem, 2, {"ctx": zd})

    def place(a, c):
        upos[pl.ds(PAD, L), cols(a, CB)] = jnp.dot(perm[...], arrived[a], preferred_element_type=F32).astype(BF16)
        return c

    lax.fori_loop(0, 3, place, 0)

    over.wait_recv()
    theirs = cotz.at[1 - x, z]
    u_oth = send(theirs, theirs, csem, 3, {"ctx": zu})
    d_oth = send(theirs, theirs, csem, 4, {"ctx": zd})

    def forward(n, carry):
        c0 = pl.multiple_of(lax.rem(n, CB // 128) * 128, 128)
        cs = pl.ds(c0, 128)
        r0 = pl.multiple_of((n // (CB // 128)) * STRIP, STRIP)
        m = mask[pl.ds(r0 + 8, STRIP + 8), :]
        made = []
        for a in range(3):
            u = upos[pl.ds(r0, STRIP + PAD), pl.ds(a * CB + c0, 128)].astype(F32)[8:]
            made.append(taps3(u, m, [short[t, pl.ds(a, 1), cs] for t in range(3)]))
        q, k, v = made
        zt = k * v
        w = inner[pl.ds(0, 1), cs] * zt
        for t in range(1, 7):
            zt = down(zt, m)
            w = w + inner[pl.ds(t, 1), cs] * zt
        for a, val in enumerate((q, k, v, w)):
            feats[a, pl.ds(r0, STRIP), cs] = val[8:].astype(BF16)
        ypos[pl.ds(r0, STRIP), cs] = (q * w)[8:].astype(BF16)
        return carry

    lax.fori_loop(0, (CB // 128) * (L // STRIP), forward, 0)
    my_y = cols(x, CB)
    y[:, my_y] = lax.dot_general(perm[...], ypos[...], TN, preferred_element_type=F32).astype(BF16)
    y_x = send(y.at[:, my_y], y.at[:, my_y], csem, 7, {"ctx": xb})

    wy[2].wait_recv()
    wy[3].wait_recv()
    ws.append(again(pair(yo), 9, sib))
    for c in ws:
        c.wait_recv()
    own_c.wait()

    def grads_of(zz):
        lhs = cotz[:, zz].reshape(2 * ROWS, HF)
        there = jnp.dot(lhs, w2[1 - x].reshape(HF, CB), preferred_element_type=F32).astype(BF16)
        here = jnp.dot(lhs, w2[x].reshape(HF, CB), preferred_element_type=F32)
        for a in range(2):
            rs = pl.ds(pl.multiple_of(a * 512 + zz * ROWS, ROWS), ROWS)
            dysend[rs, :] = there[a * ROWS : (a + 1) * ROWS]
            dypos[rs, :] = here[a * ROWS : (a + 1) * ROWS]

    d_x = []

    def send_grads(zz):
        for a in range(2):
            rs = pl.ds(pl.multiple_of(a * 512 + zz * ROWS, ROWS), ROWS)
            d_x.append(send(dysend.at[rs], dyrecv.at[rs], (d_s, d_r), len(d_x), {"ctx": xb}))

    def grads_step(n, carry):
        grads_of(lax.rem(z + 1 + 2 * n, 4))
        return carry

    grads_of(z)
    u_own.wait_recv()
    d_own.wait_recv()
    u_oth.wait_recv()
    d_oth.wait_recv()
    on_u = send(cotz.at[0, zdl], cotz.at[0, zdl], csem, 5, {"ctx": zu})
    on_d = send(cotz.at[1, zul], cotz.at[1, zul], csem, 6, {"ctx": zd})
    lax.fori_loop(0, 2, grads_step, 0)
    on_u.wait_recv()
    on_d.wait_recv()
    grads_of(zo)

    y_x.wait_recv()
    for k in (z, zul, zdl, zo):
        send_grads(k)

    def part(n, carry):
        def rows_of(b):
            return w2[b, pl.ds(n * 2, 2)].reshape(512, CB)

        val = lax.dot_general(y[:, pl.ds(0, CB)], rows_of(0), NT, preferred_element_type=F32) + lax.dot_general(
            y[:, pl.ds(CB, CB)], rows_of(1), NT, preferred_element_type=F32
        )
        for a in range(2):
            for zz in range(4):
                r0 = (a * 4 + zz) * ROWS
                parts[lax.rem(zz - z + 4, 4), a, :, cols(n, 512)] = val[r0 : r0 + ROWS].astype(BF16)
        return carry

    lax.fori_loop(0, HF // 512, part, 0)
    rsem = (r_s, r_r)
    s_u = send(parts.at[2, 0], got1.at[0], rsem, 0, {"ctx": zu})
    s_d = send(parts.at[2, 1], got1.at[1], rsem, 1, {"ctx": zd})

    vsem = (v_s, v_r)

    def weights(which, dst):
        def step(k, carry):
            lhs = cotz[:, :, :, cols(k * 2 + which, 256)].reshape(L, 256)
            val = lax.dot_general(lhs, y[...], TN, preferred_element_type=F32).astype(BF16)
            dst[k, 0] = val[:, :CB]
            dst[k, 1] = val[:, CB:]
            return carry

        lax.fori_loop(0, 4, step, 0)

    weights(1 - core, gsib)
    g_sib = send(gsib, ggot, vsem, 0, {"dp": sib})
    t_u = send(parts.at[1, 1], got2.at[0, 1], rsem, 2, {"ctx": zu})
    t_d = send(parts.at[3, 0], got2.at[1, 0], rsem, 3, {"ctx": zd})
    weights(core, gown)

    def combine(a, k):
        def fn(rs):
            fwd[a, rs, :] = (parts[k, a, rs, :].astype(F32) + got1[a, rs, :].astype(F32)).astype(BF16)

        strips(ROWS, 16, fn)

    s_u.wait_recv()
    combine(0, 1)
    f_u = send(fwd.at[0], got2.at[0, 0], rsem, 4, {"ctx": zu})
    s_d.wait_recv()
    combine(1, 3)
    f_d = send(fwd.at[1], got2.at[1, 1], rsem, 5, {"ctx": zd})

    g_sib.wait_recv()

    def add_pairs(n, carry):
        k, b = n // 2, lax.rem(n, 2)

        def fn(rs):
            gown[k, b, rs, :] = (gown[k, b, rs, :].astype(F32) + ggot[k, b, rs, :].astype(F32)).astype(BF16)

        strips(256, 64, fn)
        return carry

    lax.fori_loop(0, 8, add_pairs, 0)
    gy = [
        send(gown.at[yo, 0], ggot1.at[0], vsem, 1, {"dp": up_y}),
        send(gown.at[yo, 1], ggot1.at[1], vsem, 2, {"dp": dn_y}),
        send(gown.at[yu, 1], ggot2.at[0, 1], vsem, 3, {"dp": up_y}),
        send(gown.at[yd, 0], ggot2.at[1, 0], vsem, 4, {"dp": dn_y}),
    ]

    for c in d_x:
        c.wait_recv()

    def add_dy(rs):
        ypos[rs, :] = (dypos[rs, :] + dyrecv[rs, :].astype(F32)).astype(BF16)

    strips(L, 64, add_dy)
    dypos[pl.ds(0, L), :] = jnp.dot(perm[...], ypos[...], preferred_element_type=F32)

    def out_copy(c, n):
        p = j if n is None else peer(x, z, *A2A[n])
        src = arrived.at[:, pl.ds(pl.multiple_of(p * ROWS, ROWS), ROWS), cols(c, 128)]
        dst = dugot.at[:, :, pl.ds(pl.multiple_of(j * CB + c * 128, 128), 128)]
        if n is None:
            return pltpu.make_async_copy(src, dst, l_s.at[4 + c])
        return remote(src, dst, (q_s, q_r), c * 7 + n, {"ctx": p})

    def chunk(c, carry):
        cs = cols(c, 128)

        def backward(n, carry):
            r0 = pl.multiple_of(n * STRIP, STRIP)
            m = mask[pl.ds(r0 + PAD, STRIP + 8), :]
            q, k, v, w = [feats[a, pl.ds(r0, STRIP + PAD), cs].astype(F32)[: STRIP + 8] for a in range(4)]
            dy = dypos[pl.ds(r0, STRIP + 8), cs]

            def total(val):
                return jnp.sum(val.reshape(STRIP // 8, 8, 128), axis=0)

            b = dy * q
            zs = (k * v)[:STRIP]
            dz = inner[pl.ds(0, 1), cs] * b
            gacc[9, :, cs] += total(b[:STRIP] * zs)
            for t in range(1, 7):
                b = up(b, m)
                dz = dz + inner[pl.ds(t, 1), cs] * b
                gacc[9 + t, :, cs] += total(b[:STRIP] * zs)
            df = (dy * w, dz * v, dz * k)
            for a in range(3):
                u = upos[pl.ds(PAD + r0, STRIP), pl.ds(pl.multiple_of(a * CB + c * 128, 128), 128)].astype(F32)
                b = df[a]
                du = short[0, pl.ds(a, 1), cs] * b
                gacc[a, :, cs] += total(b[:STRIP] * u)
                for t in range(1, 3):
                    b = up(b, m)
                    du = du + short[t, pl.ds(a, 1), cs] * b
                    gacc[t * 3 + a, :, cs] += total(b[:STRIP] * u)
                dupos[pl.ds(r0, STRIP), pl.ds(a * 128, 128)] = du[:STRIP].astype(BF16)
            return carry

        lax.fori_loop(0, L // STRIP, backward, 0)
        val = lax.dot_general(perm[...], dupos[...], TN, preferred_element_type=F32).astype(BF16)
        for a in range(3):
            arrived[a, :, cs] = val[:, a * 128 : (a + 1) * 128]
        for n in range(7):
            out_copy(c, n).start()
        out_copy(c, None).start()
        return carry

    lax.fori_loop(0, 2, chunk, 0)
    gy[0].wait_recv()
    gy[1].wait_recv()
    for a, k in ((0, yu), (1, yd)):

        def add_fwd(rs):
            gfwd[a, rs, :] = (gown[k, a, rs, :].astype(F32) + ggot1[a, rs, :].astype(F32)).astype(BF16)

        strips(256, 64, add_fwd)
    gy.append(send(gfwd.at[0], ggot2.at[0, 0], vsem, 5, {"dp": up_y}))
    gy.append(send(gfwd.at[1], ggot2.at[1, 1], vsem, 6, {"dp": dn_y}))
    lax.fori_loop(2, 4, chunk, 0)

    for k in range(16):
        gall[0, pl.ds(k, 1), :] = jnp.sum(gacc[k], axis=0, keepdims=True)
    near_y = dp_id(h, yy + 1 - 2 * lax.rem(yy, 2), core)
    gx = []

    def exchange(n):
        gx.append(send(gall.at[2 * n], gall.at[2 * n + 1], (g_s, g_r), n, {"dp": (sib, near_y, over_y, flip)[n]}))

    def summed(n):
        gx[n].wait_recv()
        gall[2 * n + 2] = gall[2 * n] + gall[2 * n + 1]

    exchange(0)

    for cp in (t_u, t_d, f_u, f_d):
        cp.wait_recv()

    def finish(a, dst):
        def fn(rs):
            final[dst, rs, :] = (
                parts[0, a, rs, :].astype(F32) + (got2[0, a, rs, :].astype(F32) + got2[1, a, rs, :].astype(F32))
            ).astype(BF16)

        strips(ROWS, 16, fn)

    finish(1 - x, 0)
    m_x = send(final.at[0], mixed.at[:, cols(x, HF)], rsem, 6, {"ctx": xb})
    summed(0)
    exchange(1)
    finish(x, 1)
    m_own = pltpu.make_async_copy(final.at[1], mixed.at[:, cols(x, HF)], l_s.at[2])
    m_own.start()

    for k in range(2, 6):
        gy[k].wait_recv()
    for a in range(2):

        def add_all(rs):
            gred[a, rs, :] = (
                gown[yy, a, rs, :].astype(F32) + (ggot2[0, a, rs, :].astype(F32) + ggot2[1, a, rs, :].astype(F32))
            ).astype(BF16)

        strips(256, 64, add_all)

    def owner_copy(a):
        return remote(gred.at[a], gfin.at[h], vsem, 7 + a, {"dp": dp_id(x, yy, core), "ctx": a * 4 + z}, 7 + h)

    for a in range(2):

        @pl.when((h != x) | (x != a))
        def _():
            owner_copy(a).start()

    @pl.when(h == x)
    def _():
        def keep(rs):
            gfin[h, rs, :] = gred[x, rs, :]

        strips(256, 64, keep)

    summed(1)
    exchange(2)
    summed(2)
    exchange(3)
    summed(3)
    sums = gall[8]
    for t in range(3):
        short_out[t] = sums[t * 3 : t * 3 + 3]
    inner_out[...] = lax.dot_general(
        sums[9:16], spread, NT, preferred_element_type=F32, precision=lax.Precision.HIGHEST
    )

    for s in range(2):

        @pl.when((h != x) | (h != s))
        def _():
            remote(gred.at[0], gfin.at[s], vsem, 7, {"ctx": xb}, 7 + s).wait_recv()

    def last(rs):
        gw_out[rs, :] = gfin[0, rs, :].astype(F32) + gfin[1, rs, :].astype(F32)

    strips(256, 64, last)

    for a in range(2):

        @pl.when((h != x) | (x != a))
        def _():
            owner_copy(a).wait_send()

    @pl.when(h != x)
    def _():
        w_b.wait_send()

    m_own.wait()
    m_x.wait()
    for cp in (w_a, *wy, *ws, *a_in, over, u_own, d_own, u_oth, d_oth, on_u, on_d, y_x, *d_x):
        cp.wait_send()
    for cp in (s_u, s_d, t_u, t_d, f_u, f_d, g_sib, *gy, *gx):
        cp.wait_send()
    for c in range(4):
        for n in (*range(7), None):
            out_copy(c, n).wait()


VM = pl.BlockSpec(memory_space=pltpu.VMEM)
SM = pl.BlockSpec(memory_space=pltpu.SMEM)
HB = pl.BlockSpec(memory_space=pl.ANY)
DMA = pltpu.SemaphoreType.DMA
NT = (((1,), (1,)), ((), ()))
TN = (((0,), (0,)), ((), ()))


def sems(*counts):
    return [DMA((n,)) for n in counts for _ in range(2)]


def block(qs, cot, wt, order_row, lens, short, inner):
    sds = jax.ShapeDtypeStruct
    vm = pltpu.VMEM
    return pl.pallas_call(
        block_kernel,
        out_shape=(
            sds((ROWS, 2 * HF), BF16),
            sds((3, ROWS, 8 * CB), BF16),
            sds((256, CB), F32),
            sds((3, 3, CB), F32),
            sds((7, CB // GROUP), F32),
        ),
        in_specs=[HB, HB, HB, VM, SM, VM, VM],
        out_specs=(HB, HB, VM, VM, VM),
        scratch_shapes=[
            vm((3, L, CB), BF16),
            vm((L + 2 * PAD, 3 * CB), BF16),
            vm((4, L + PAD, CB), BF16),
            vm((L, L), BF16),
            vm((L + 2 * PAD, 128), F32),
            vm((L, CB), BF16),
            vm((L, 2 * CB), BF16),
            vm((2, 4, ROWS, HF), BF16),
            vm((2, 8, 256, CB), BF16),
            vm((7, CB), F32),
            vm((L, CB), BF16),
            vm((L, CB), BF16),
            vm((L + 8, CB), F32),
            vm((L, 384), BF16),
            vm((4, 2, ROWS, HF), BF16),
            vm((2, ROWS, HF), BF16),
            vm((2, ROWS, HF), BF16),
            vm((2, 2, ROWS, HF), BF16),
            vm((2, ROWS, HF), BF16),
            vm((16, 8, CB), F32),
            vm((9, 16, CB), F32),
            vm((4, 2, 256, CB), BF16),
            vm((4, 2, 256, CB), BF16),
            vm((4, 2, 256, CB), BF16),
            vm((2, 256, CB), BF16),
            vm((2, 256, CB), BF16),
            vm((2, 2, 256, CB), BF16),
            vm((2, 256, CB), BF16),
            vm((2, 256, CB), BF16),
            *sems(7, 8, 10, 7, 28, 4, 9, 8),
            DMA((8,)),
        ],
        compiler_params=pltpu.CompilerParams(collective_id=0, has_side_effects=True, vmem_limit_bytes=60 << 20),
        cost_estimate=pl.CostEstimate(flops=30 << 30, bytes_accessed=100 << 20, transcendentals=0),
        name="block",
    )(qs, cot, wt, order_row, lens, short, inner)


def on_device(qkv, short_filter, inner_filter, out_weight, cotangent, order, lengths):
    qs = qkv.transpose(1, 0, 2)
    mixed, dugot, gw, grad_short, grad_inner = block(
        qs, cotangent, out_weight, order, lengths, short_filter, inner_filter
    )
    return (mixed, dugot.transpose(1, 0, 2), gw, grad_short, grad_inner)


def solution(mesh):
    in_specs = (
        P(("dp", "ctx"), None, None),
        P(None, None, "ctx"),
        P(None, "ctx"),
        P("dp", "ctx"),
        P(("dp", "ctx"), None),
        P("dp", None),
        P("dp", None),
    )
    out_specs = (
        P(("dp", "ctx"), None),
        P(("dp", "ctx"), None, None),
        P("dp", "ctx"),
        P(None, None, "ctx"),
        P(None, "ctx"),
    )
    return jax.shard_map(on_device, mesh=mesh, in_specs=in_specs, out_specs=out_specs, check_vma=False)
```
